32 devices in a mesh: groups: 1, row: 16 (over z, y, core), col: 2 (over x).
Axes of the slice: x: 2, y: 2, z: 4, core: 2. Of those that a mesh axis runs over, the one named last changes fastest.
Arguments:
- alignment_embedding: bfloat16 [32, 768, 256], P('groups', ('row', 'col')), may hold values from -6 to 6
- normalizer_factor: float32 [256], replicated, may hold values from 0.1 to 1.9
- normalizer_shift: float32 [256], replicated, may hold values from -3 to 3
- first_factor_matrix: bfloat16 [256, 32], replicated, may hold values from -0.375 to 0.375
- first_factor_shift: float32 [32], replicated, may hold values from -3 to 3
- second_factor_matrix: bfloat16 [256, 32], replicated, may hold values from -0.375 to 0.375
- second_factor_shift: float32 [32], replicated, may hold values from -3 to 3
- final_matrix: bfloat16 [1024, 128], replicated, may hold values from -1 to 1
- final_shift: float32 [128], replicated, may hold values from -3 to 3
Outputs:
- pair_update: bfloat16 [768, 768, 128], P(('groups', 'row'), 'col')
The draws below stay inside these ranges and needn't reach their ends.
All inputs are finite; a program needn't handle non-finite values.
Results may differ from the reference program's by a relative error of at most 0.0056.
Values may be sent and summed in bfloat16 or wider, within the bound.
No kernel may reach another device: no remote copies, remote signals or barrier semaphores. Data moves between devices by JAX's collectives and lax.ppermute only.
A program may use at most 64 MiB of HBM per device.

```python
import jax
import jax.numpy as jnp
from jax import lax

ALIGN_FEATURES = 256
HIDDEN_WIDTH = 32
CZ = 128
ALIGNED_HOMOLOGS = 32
RES_DEV = 48
CHAIN_POSITIONS = 768


def shard_levels(own_key, extent, pieces, least, top_value):
    gain = 1.0
    for position, parts in pieces:
        draws = jax.random.uniform(jax.random.fold_in(jax.random.fold_in(own_key, 6), position), (parts,), jnp.float32, least / len(pieces), top_value / len(pieces))
        gain = gain * jnp.repeat(jnp.exp(draws), extent[position] // parts).reshape((-1,) + (1,) * (len(extent) - 1 - position))
    return gain


def normal_values(key, extent, deviation, limit, pieces=(), dtype=jnp.bfloat16):
    result = deviation * jax.random.normal(key, extent, jnp.float32)
    if pieces:
        result = result * shard_levels(key, extent, pieces, -0.22, 0.18)
    return jnp.clip(result, -limit, limit).astype(dtype)


def setup_inputs(seed: int = 0, part: int = 0) -> dict:
    key_of = jax.random.split(jax.random.key(seed), 10)
    part_splits = jax.random.split(jax.random.fold_in(key_of[9], part), 10)
    alignment_embedding = normal_values(part_splits[0], (ALIGNED_HOMOLOGS, CHAIN_POSITIONS, ALIGN_FEATURES), 1.0, 6.0, ((1, 32),))
    normalizer_factor = jnp.clip(1.0 + 0.18 * jax.random.normal(key_of[1], (ALIGN_FEATURES,), jnp.float32), 0.1, 1.9)
    normalizer_shift = normal_values(key_of[2], (ALIGN_FEATURES,), 0.5, 3.0, (), jnp.float32)
    first_factor_matrix = normal_values(key_of[3], (ALIGN_FEATURES, HIDDEN_WIDTH), ALIGN_FEATURES ** -0.5, 0.375)
    first_factor_shift = normal_values(key_of[4], (HIDDEN_WIDTH,), 0.5, 3.0, (), jnp.float32)
    second_factor_matrix = normal_values(key_of[5], (ALIGN_FEATURES, HIDDEN_WIDTH), ALIGN_FEATURES ** -0.5, 0.375)
    second_factor_shift = normal_values(key_of[6], (HIDDEN_WIDTH,), 0.5, 3.0, (), jnp.float32)
    final_matrix = normal_values(key_of[7], (HIDDEN_WIDTH * HIDDEN_WIDTH, CZ), HIDDEN_WIDTH ** -0.5, 1.0)
    final_shift = normal_values(key_of[8], (CZ,), 0.5, 3.0, (), jnp.float32)
    return dict(alignment_embedding=alignment_embedding, normalizer_factor=normalizer_factor, normalizer_shift=normalizer_shift, first_factor_matrix=first_factor_matrix, first_factor_shift=first_factor_shift, second_factor_matrix=second_factor_matrix, second_factor_shift=second_factor_shift, final_matrix=final_matrix, final_shift=final_shift)


def reference(alignment_embedding, normalizer_factor, normalizer_shift, first_factor_matrix, first_factor_shift, second_factor_matrix, second_factor_shift, final_matrix, final_shift):
    element_numbers = alignment_embedding.astype(jnp.float32)
    average = lax.optimization_barrier(jnp.mean(element_numbers, axis=-1, keepdims=True))
    centered = element_numbers - average
    variance = lax.optimization_barrier(jnp.mean(centered * centered, axis=-1, keepdims=True))
    normed = (centered * lax.rsqrt(variance + 1e-05) * normalizer_factor + normalizer_shift).astype(jnp.bfloat16)
    normed_wide = normed.astype(jnp.float32)
    left_proj = (jnp.einsum('src,ck->srk', normed_wide, first_factor_matrix.astype(jnp.float32)) + first_factor_shift).astype(jnp.bfloat16)
    right_proj = (jnp.einsum('src,ck->srk', normed_wide, second_factor_matrix.astype(jnp.float32)) + second_factor_shift).astype(jnp.bfloat16)
    seq_count = left_proj.shape[0]
    res_total = left_proj.shape[1]
    width = left_proj.shape[2]
    block_count = res_total // RES_DEV
    left_blocks = left_proj.reshape(seq_count, block_count, RES_DEV, width).transpose(1, 0, 2, 3)
    right_wide = right_proj.astype(jnp.float32)
    out_wide = final_matrix.astype(jnp.float32)

    def one_block(left_block):
        outer = jnp.einsum('sic,sjd->ijcd', left_block.astype(jnp.float32), right_wide) / seq_count
        outer = outer.astype(jnp.bfloat16).reshape(RES_DEV, res_total, width * width)
        update = jnp.einsum('ijk,ke->ije', outer.astype(jnp.float32), out_wide) + final_shift
        return update.astype(jnp.bfloat16)
    tiles = lax.map(one_block, left_blocks)
    return tiles.reshape(res_total, res_total, -1)
```

```python
import functools

import jax
import jax.numpy as jnp
from jax import lax
from jax.experimental import pallas as pl
from jax.experimental.pallas import tpu as pltpu
from jax.sharding import PartitionSpec as P

F32, BF16 = jnp.float32, jnp.bfloat16
LANES = 128
RUN = 8


def project_kernel(*refs):
    sources, (r_ref, l_ref, held), buffers, sems = refs[:7], refs[7:10], refs[10:17], refs[17]
    copies = [pltpu.make_async_copy(src, dst, sems.at[k]) for k, (src, dst) in enumerate(zip(sources, buffers))]
    for copy in copies:
        copy.start()
    for copy in copies:
        copy.wait()
    x_ref, gain_ref, shift_ref, left_ref, left_shift_ref, right_ref, right_shift_ref = buffers
    seqs, here, channels = x_ref.shape
    width = left_ref.shape[0]
    groups = LANES // width
    x = x_ref[...].astype(F32).reshape(seqs * here, channels)
    centered = x - jnp.mean(x, axis=-1, keepdims=True)
    variance = jnp.mean(centered * centered, axis=-1, keepdims=True)
    normed = (centered * lax.rsqrt(variance + 1e-05) * gain_ref[...] + shift_ref[...]).astype(BF16)
    matrices = jnp.concatenate([left_ref[...]] * groups + [right_ref[...]] * groups, axis=0)
    shifts = jnp.concatenate([left_shift_ref[...]] * groups + [right_shift_ref[...]] * groups, axis=1)
    both = lax.dot_general(normed, matrices, (((1,), (1,)), ((), ())), preferred_element_type=F32) + shifts
    held[0], held[1] = both[:, :LANES], both[:, LANES:]
    group = lax.broadcasted_iota(jnp.int32, (1, LANES), 1) // width
    per = here // groups
    for i in range(per):
        packed = held[0, pl.ds(i, seqs, stride=here), :]
        for g in range(1, groups):
            packed = jnp.where(group == g, held[0, pl.ds(g * per + i, seqs, stride=here), :], packed)
        l_ref[i * seqs : (i + 1) * seqs, :] = packed.astype(BF16)
    rows = []
    for q in range(seqs // RUN):
        tiles = []
        for t in range(RUN // groups):
            s = q * RUN + t * groups
            packed = held[1, s * here : (s + 1) * here, :]
            for g in range(1, groups):
                packed = jnp.where(group == g, held[1, (s + g) * here : (s + g + 1) * here, :], packed)
            tiles.append(packed)
        rows.append(jnp.concatenate(tiles, axis=1))
    packed = jnp.concatenate(rows, axis=0).astype(BF16)
    span = RUN * width
    a = lax.broadcasted_iota(jnp.int32, (span, span), 0)
    b = lax.broadcasted_iota(jnp.int32, (span, span), 1)
    order = jnp.where((a % width) * RUN + a // width == b, 1.0, 0.0).astype(BF16)
    ordered = jnp.dot(packed, order, preferred_element_type=F32).astype(BF16)
    for q in range(seqs // RUN):
        r_ref[:, q * span : (q + 1) * span] = ordered[q * here : (q + 1) * here, :]


def spread_left(seqs, width, l_ref, pairs, t_ref):
    groups = LANES // width
    residues = l_ref.shape[0] // seqs * groups
    left = jnp.concatenate([l_ref[:, g * width : (g + 1) * width] for g in range(groups)], axis=0)
    unroll = 4

    def step(n, carry):
        for u in range(unroll):
            m = n * unroll + u
            wide_out = jnp.dot(left, pairs[m], preferred_element_type=F32)
            for i in range(residues):
                for q in range(seqs // RUN):
                    s = i * seqs + q * RUN
                    block = jnp.concatenate([wide_out[s : s + RUN, :LANES], wide_out[s : s + RUN, LANES:]], axis=0)
                    start = pl.multiple_of(q * RUN * width + m * 2 * RUN, 2 * RUN)
                    t_ref[i // 2, pl.ds(start, 2 * RUN), (i % 2) * LANES : (i % 2 + 1) * LANES] = block.astype(BF16)
        return carry

    lax.fori_loop(0, width // 2 // unroll, step, 0)


def spread_first_kernel(seqs, width, l_ref, f_ref, t_ref, pairs, wide):
    wide[...] = f_ref[...].astype(F32)
    for d in range(width):
        pairs[d // 2, :, (d % 2) * LANES : (d % 2 + 1) * LANES] = wide[pl.ds(d, width, stride=width), :].astype(BF16)
    spread_left(seqs, width, l_ref, pairs, t_ref)


def spread_second_kernel(seqs, width, l_ref, pairs, t_ref):
    spread_left(seqs, width, l_ref, pairs, t_ref)


def arrange_kernel(own_ref, near_ref, far_ref, _, pair_ref):
    row, col = lax.axis_index("row"), lax.axis_index("col")
    inside = row // 8 == col
    here = own_ref.shape[0]
    own, near, far = own_ref[...], near_ref[...], far_ref[...]
    same, other = jnp.where(inside, own, near), jnp.where(inside, near, far)
    pair_ref[:here, :] = jnp.where(col == 0, same, other)
    pair_ref[here:, :] = jnp.where(col == 0, other, same)


def combine_kernel(seqs, masks, n_left, *refs):
    lefts, pieces = refs[:n_left], refs[n_left : n_left + len(masks)]
    shift_ref, out_ref, right, stage, sem = refs[n_left + len(masks) :]
    rows = pieces[0].shape[0]
    pairs = lefts[0].shape[0]
    for mask, piece in zip(masks, pieces):
        place = jnp.bitwise_xor(lax.rem(lax.axis_index("row"), len(masks)), mask) if len(masks) > 1 else 0
        right[pl.ds(pl.multiple_of(place * rows, rows), rows), :] = piece[...]
    shift = jnp.concatenate([shift_ref[...]] * 2, axis=1)
    unroll = next(u for u in (6, 4, 3, 2, 1) if pairs % u == 0)

    for h, left in enumerate(lefts):
        first = 2 * pairs * (jnp.bitwise_xor(lax.axis_index("col"), h) if n_left > 1 else 0)

        def step(n, carry, left=left, first=first, h=h):
            for u in range(unroll):
                p = n * unroll + u
                update = jnp.dot(right[...], left[p], preferred_element_type=F32) * (1.0 / seqs) + shift
                stage[h * pairs + p, 0] = update[:, :LANES].astype(BF16)
                stage[h * pairs + p, 1] = update[:, LANES:].astype(BF16)
                pltpu.make_async_copy(stage.at[h * pairs + p], out_ref.at[pl.ds(first + 2 * p, 2)], sem.at[h * pairs + p]).start()
            return carry

        lax.fori_loop(0, pairs // unroll, step, 0)

    def wait(p, carry):
        pltpu.make_async_copy(stage.at[p], out_ref.at[pl.ds(2 * p, 2)], sem.at[p]).wait()
        return carry

    lax.fori_loop(0, n_left * pairs, wait, 0)


VMEM = pl.BlockSpec(memory_space=pltpu.VMEM)
HBM = pl.BlockSpec(memory_space=pltpu.HBM)


def params():
    return pltpu.CompilerParams(vmem_limit_bytes=12 << 20)


def keep(value):
    return pltpu.with_memory_space_constraint(value, pltpu.VMEM)


def project(x, gain, shift, first, first_shift, second, second_shift):
    seqs, here, channels = x.shape
    width = first.shape[1]
    args = (x, gain[None], shift[None], first.T, first_shift[None], second.T, second_shift[None])
    args = [pltpu.with_memory_space_constraint(a, pltpu.HBM) for a in args]
    return pl.pallas_call(
        project_kernel,
        out_shape=(
            jax.ShapeDtypeStruct((here, seqs * width), BF16),
            jax.ShapeDtypeStruct((here * width // LANES * seqs, LANES), BF16),
        ),
        in_specs=[HBM] * len(args),
        out_specs=(VMEM, VMEM),
        scratch_shapes=[pltpu.VMEM((2, seqs * here, LANES), F32)]
        + [pltpu.VMEM(a.shape, a.dtype) for a in args]
        + [pltpu.SemaphoreType.DMA((len(args),))],
        compiler_params=params(),
        cost_estimate=pl.CostEstimate(flops=2 * x.size * 256, bytes_accessed=2 * x.size, transcendentals=0),
        name="project",
    )(*args)


def spread(left, final, seqs, width, pairs=None):
    residues = left.shape[0] // seqs * (LANES // width)
    wide = pltpu.VMEM((residues // 2, seqs * width, 2 * LANES), BF16)
    cost = pl.CostEstimate(
        flops=2 * residues * seqs * 256 * width * LANES, bytes_accessed=left.size * 2, transcendentals=0
    )
    if pairs is None:
        return pl.pallas_call(
            functools.partial(spread_first_kernel, seqs, width),
            out_shape=(wide, pltpu.VMEM((width // 2, width, 2 * LANES), BF16)),
            in_specs=[VMEM] * 2,
            out_specs=(VMEM, VMEM),
            scratch_shapes=[pltpu.VMEM(final.shape, F32)],
            compiler_params=params(),
            cost_estimate=cost,
            name="spread_first",
        )(left, final)
    return pl.pallas_call(
        functools.partial(spread_second_kernel, seqs, width),
        out_shape=wide,
        in_specs=[VMEM] * 2,
        out_specs=VMEM,
        compiler_params=params(),
        cost_estimate=cost,
        name="spread_second",
    )(left, keep(pairs))


def arrange(own, near, far, after):
    return pl.pallas_call(
        arrange_kernel,
        out_shape=jax.ShapeDtypeStruct((2 * own.shape[0], own.shape[1]), BF16),
        in_specs=[VMEM] * 4,
        out_specs=VMEM,
        compiler_params=params(),
        name="arrange",
    )(own, near, far, keep(after))


def combine(lefts, pieces, masks, final_shift, seqs):
    pairs, depth, _ = lefts[0].shape
    span = pieces[0].shape[0] * len(pieces)
    total = 2 * pairs * len(lefts)
    return pl.pallas_call(
        functools.partial(combine_kernel, seqs, masks, len(lefts)),
        out_shape=jax.ShapeDtypeStruct((total, span, LANES), BF16),
        in_specs=[VMEM] * (len(lefts) + len(pieces) + 1),
        out_specs=HBM,
        scratch_shapes=[
            pltpu.VMEM((span, depth), BF16),
            pltpu.VMEM((total // 2, 2, span, LANES), BF16),
            pltpu.SemaphoreType.DMA((total // 2,)),
        ],
        compiler_params=params(),
        cost_estimate=pl.CostEstimate(
            flops=2 * total * span * LANES * depth, bytes_accessed=total * span * LANES * 2, transcendentals=0
        ),
        name="combine",
    )(*[keep(left) for left in lefts], *pieces, final_shift[None])


def linear(target):
    moves = []
    for r in range(16):
        for c in range(2):
            t = target(r, c, r // 8 == c)
            if t is not None:
                moves.append((r * 2 + c, t[0] * 2 + t[1]))
    return moves


def flip(value, bits):
    return lax.ppermute(value, "row", [(r, r ^ bits) for r in range(16)])


def plain(x, gain, shift, first, first_shift, second, second_shift, final, final_shift):
    seqs, here, _ = x.shape
    width = first.shape[1]
    wide = x.astype(F32)
    centered = wide - jnp.mean(wide, axis=-1, keepdims=True)
    variance = jnp.mean(centered * centered, axis=-1, keepdims=True)
    normed = (centered * lax.rsqrt(variance + 1e-05) * gain + shift).astype(BF16)
    left = (jnp.einsum("src,ck->rsk", normed, first, preferred_element_type=F32) + first_shift).astype(BF16)
    right = (jnp.einsum("src,ck->rks", normed, second, preferred_element_type=F32) + second_shift).astype(BF16)
    right = right.reshape(here, width, seqs // RUN, RUN).transpose(0, 2, 1, 3).reshape(here, seqs * width)
    left = lax.all_gather(left.reshape(here, seqs * width), "col", axis=0, tiled=True)
    groups = LANES // width
    left = left.reshape(groups, -1, width).transpose(1, 0, 2).reshape(-1, LANES)
    every = lax.all_gather(right, ("row", "col"), axis=0, tiled=True)
    span = every.shape[0] // lax.axis_size("col")
    mine = lax.dynamic_slice_in_dim(every, lax.axis_index("col") * span, span, 0)
    spread_left, _ = spread(left, final, seqs, width)
    return combine([spread_left], [mine], (0,), final_shift, seqs)


def per_device(x, gain, shift, first, first_shift, second, second_shift, final, final_shift):
    seqs, here, _ = x.shape
    width = first.shape[1]
    if (lax.axis_size("row"), lax.axis_size("col"), here % 24) != (16, 2, 0):
        return plain(x, gain, shift, first, first_shift, second, second_shift, final, final_shift)
    right, left = project(x, gain, shift, first, first_shift, second, second_shift)
    both = ("row", "col")
    far = lax.ppermute(right, both, linear(lambda r, c, i: None if i else (r ^ 8, 1 - c)))
    beside = lax.ppermute(left, "col", [(0, 1), (1, 0)])
    near = lax.ppermute(right, both, linear(lambda r, c, i: (r ^ 8, c) if i else (r, 1 - c)))
    own, pairs = spread(left, final, seqs, width)
    pair = arrange(right, near, far, pairs)
    pieces = [pair] + [flip(pair, bits) for bits in (2, 4, 6)]
    pieces += [flip(piece, 1) for piece in pieces]
    lefts = [own, spread(beside, final, seqs, width, pairs)]
    return combine(lefts, pieces, (0, 2, 4, 6, 1, 3, 5, 7), final_shift, seqs)


def solution(mesh):
    return jax.shard_map(
        per_device,
        mesh=mesh,
        in_specs=(P("groups", ("row", "col"), None), P(), P(), P(), P(), P(), P(), P(), P()),
        out_specs=P(("groups", "row"), "col", None),
        check_vma=False,
    )
```

```python
import functools

import jax
import jax.numpy as jnp
from jax import lax
from jax.experimental import pallas as pl
from jax.experimental.pallas import tpu as pltpu
from jax.sharding import PartitionSpec as P

F32, BF16 = jnp.float32, jnp.bfloat16
LANES = 128
RUN = 8


def project_kernel(*refs):
    sources, (r_ref, l_ref, final_ref, held), buffers, sems = refs[:8], refs[8:12], refs[12:19], refs[19]
    targets = (*buffers, final_ref)
    copies = [pltpu.make_async_copy(src, dst, sems.at[k]) for k, (src, dst) in enumerate(zip(sources, targets))]
    for copy in copies:
        copy.start()
    for copy in copies[:-1]:
        copy.wait()
    x_ref, gain_ref, shift_ref, left_ref, left_shift_ref, right_ref, right_shift_ref = buffers
    seqs, here, channels = x_ref.shape
    width = left_ref.shape[0]
    groups = LANES // width
    x = x_ref[...].astype(F32).reshape(seqs * here, channels)
    centered = x - jnp.mean(x, axis=-1, keepdims=True)
    variance = jnp.mean(centered * centered, axis=-1, keepdims=True)
    normed = (centered * lax.rsqrt(variance + 1e-05) * gain_ref[...] + shift_ref[...]).astype(BF16)
    matrices = jnp.concatenate([left_ref[...]] * groups + [right_ref[...]] * groups, axis=0)
    shifts = jnp.concatenate([left_shift_ref[...]] * groups + [right_shift_ref[...]] * groups, axis=1)
    both = lax.dot_general(normed, matrices, (((1,), (1,)), ((), ())), preferred_element_type=F32) + shifts
    held[0], held[1] = both[:, :LANES], both[:, LANES:]
    group = lax.broadcasted_iota(jnp.int32, (1, LANES), 1) // width
    per = here // groups
    for i in range(per):
        packed = held[0, pl.ds(i, seqs, stride=here), :]
        for g in range(1, groups):
            packed = jnp.where(group == g, held[0, pl.ds(g * per + i, seqs, stride=here), :], packed)
        l_ref[i * seqs : (i + 1) * seqs, :] = packed.astype(BF16)
    rows = []
    for q in range(seqs // RUN):
        tiles = []
        for t in range(RUN // groups):
            s = q * RUN + t * groups
            packed = held[1, s * here : (s + 1) * here, :]
            for g in range(1, groups):
                packed = jnp.where(group == g, held[1, (s + g) * here : (s + g + 1) * here, :], packed)
            tiles.append(packed)
        rows.append(jnp.concatenate(tiles, axis=1))
    packed = jnp.concatenate(rows, axis=0).astype(BF16)
    span = RUN * width
    a = lax.broadcasted_iota(jnp.int32, (span, span), 0)
    b = lax.broadcasted_iota(jnp.int32, (span, span), 1)
    order = jnp.where((a % width) * RUN + a // width == b, 1.0, 0.0).astype(BF16)
    ordered = jnp.dot(packed, order, preferred_element_type=F32).astype(BF16)
    for q in range(seqs // RUN):
        r_ref[:, q * span : (q + 1) * span] = ordered[q * here : (q + 1) * here, :]
    copies[-1].wait()


def spread_left(seqs, width, l_ref, pairs, t_ref):
    groups = LANES // width
    residues = l_ref.shape[0] // seqs * groups
    left = jnp.concatenate([l_ref[:, g * width : (g + 1) * width] for g in range(groups)], axis=0)
    for m in range(width // 2):
        wide_out = jnp.dot(left, pairs[m], preferred_element_type=F32)
        for i in range(residues):
            for q in range(seqs // RUN):
                s = i * seqs + q * RUN
                block = jnp.concatenate([wide_out[s : s + RUN, :LANES], wide_out[s : s + RUN, LANES:]], axis=0)
                start = q * RUN * width + m * 2 * RUN
                t_ref[i // 2, start : start + 2 * RUN, (i % 2) * LANES : (i % 2 + 1) * LANES] = block.astype(BF16)


def spread_first_kernel(seqs, width, l_ref, f_ref, t_ref, pairs, wide):
    wide[...] = f_ref[...].astype(F32)
    for d in range(width):
        pairs[d // 2, :, (d % 2) * LANES : (d % 2 + 1) * LANES] = wide[pl.ds(d, width, stride=width), :].astype(BF16)
    spread_left(seqs, width, l_ref, pairs, t_ref)


def spread_second_kernel(seqs, width, l_ref, pairs, t_ref):
    spread_left(seqs, width, l_ref, pairs, t_ref)


def arrange_kernel(own_ref, near_ref, far_ref, _, pair_ref):
    row, col = lax.axis_index("row"), lax.axis_index("col")
    inside = row // 8 == col
    here = own_ref.shape[0]
    own, near, far = own_ref[...], near_ref[...], far_ref[...]
    same, other = jnp.where(inside, own, near), jnp.where(inside, near, far)
    pair_ref[:here, :] = jnp.where(col == 0, same, other)
    pair_ref[here:, :] = jnp.where(col == 0, other, same)


def order_kernel(*refs):
    pass


def combine_kernel(seqs, masks, n_left, *refs):
    lefts, pieces = refs[:n_left], refs[n_left : n_left + len(masks)]
    shift_ref, out_ref, right, stage, sem = refs[n_left + len(masks) :]
    rows = pieces[0].shape[0]
    pairs = lefts[0].shape[0]
    for mask, piece in zip(masks, pieces):
        place = jnp.bitwise_xor(lax.rem(lax.axis_index("row"), len(masks)), mask) if len(masks) > 1 else 0
        right[pl.ds(pl.multiple_of(place * rows, rows), rows), :] = piece[...]
    shift = jnp.concatenate([shift_ref[...]] * 2, axis=1)
    unroll = next(u for u in (12, 6, 4, 3, 2, 1) if pairs % u == 0)

    for h, left in enumerate(lefts):
        first = 2 * pairs * (jnp.bitwise_xor(lax.axis_index("col"), h) if n_left > 1 else 0)

        def step(n, carry, left=left, first=first, h=h):
            for u in range(unroll):
                p = n * unroll + u
                update = jnp.dot(right[...], left[p], preferred_element_type=F32) * (1.0 / seqs) + shift
                stage[h * pairs + p, 0] = update[:, :LANES].astype(BF16)
                stage[h * pairs + p, 1] = update[:, LANES:].astype(BF16)
                pltpu.make_async_copy(stage.at[h * pairs + p], out_ref.at[pl.ds(first + 2 * p, 2)], sem.at[h * pairs + p]).start()
            return carry

        lax.fori_loop(0, pairs // unroll, step, 0)

    def wait(p, carry):
        pltpu.make_async_copy(stage.at[p], out_ref.at[pl.ds(2 * p, 2)], sem.at[p]).wait()
        return carry

    lax.fori_loop(0, n_left * pairs, wait, 0)


VMEM = pl.BlockSpec(memory_space=pltpu.VMEM)
HBM = pl.BlockSpec(memory_space=pltpu.HBM)


def params():
    return pltpu.CompilerParams(vmem_limit_bytes=12 << 20)


def keep(value):
    return pltpu.with_memory_space_constraint(value, pltpu.VMEM)


def project(x, gain, shift, first, first_shift, second, second_shift, final):
    seqs, here, channels = x.shape
    width = first.shape[1]
    args = (x, gain[None], shift[None], first.T, first_shift[None], second.T, second_shift[None], final)
    args = [pltpu.with_memory_space_constraint(a, pltpu.HBM) for a in args]
    return pl.pallas_call(
        project_kernel,
        out_shape=(
            jax.ShapeDtypeStruct((here, seqs * width), BF16),
            jax.ShapeDtypeStruct((here * width // LANES * seqs, LANES), BF16),
            pltpu.VMEM(final.shape, BF16),
        ),
        in_specs=[HBM] * len(args),
        out_specs=(VMEM, VMEM, VMEM),
        scratch_shapes=[pltpu.VMEM((2, seqs * here, LANES), F32)]
        + [pltpu.VMEM(a.shape, a.dtype) for a in args[:-1]]
        + [pltpu.SemaphoreType.DMA((len(args),))],
        compiler_params=params(),
        cost_estimate=pl.CostEstimate(flops=2 * x.size * 256, bytes_accessed=2 * x.size, transcendentals=0),
        name="project",
    )(*args)


def spread(left, final, seqs, width, pairs=None):
    residues = left.shape[0] // seqs * (LANES // width)
    wide = pltpu.VMEM((residues // 2, seqs * width, 2 * LANES), BF16)
    cost = pl.CostEstimate(
        flops=2 * residues * seqs * 256 * width * LANES, bytes_accessed=left.size * 2, transcendentals=0
    )
    if pairs is None:
        return pl.pallas_call(
            functools.partial(spread_first_kernel, seqs, width),
            out_shape=(wide, pltpu.VMEM((width // 2, width, 2 * LANES), BF16)),
            in_specs=[VMEM] * 2,
            out_specs=(VMEM, VMEM),
            scratch_shapes=[pltpu.VMEM(final.shape, F32)],
            compiler_params=params(),
            cost_estimate=cost,
            name="spread_first",
        )(left, keep(final))
    return pl.pallas_call(
        functools.partial(spread_second_kernel, seqs, width),
        out_shape=wide,
        in_specs=[VMEM] * 2,
        out_specs=VMEM,
        compiler_params=params(),
        cost_estimate=cost,
        name="spread_second",
    )(left, keep(pairs))


def arrange(own, near, far, after):
    return pl.pallas_call(
        arrange_kernel,
        out_shape=jax.ShapeDtypeStruct((2 * own.shape[0], own.shape[1]), BF16),
        in_specs=[VMEM] * 4,
        out_specs=VMEM,
        compiler_params=params(),
        name="arrange",
    )(own, near, far, keep(after))


def after(values, *earlier):
    n = len(values)
    return pl.pallas_call(
        order_kernel,
        out_shape=[jax.ShapeDtypeStruct(v.shape, v.dtype) for v in values],
        in_specs=[pl.BlockSpec(memory_space=pl.ANY)] * (n + len(earlier)),
        out_specs=[pl.BlockSpec(memory_space=pl.ANY)] * n,
        input_output_aliases={k: k for k in range(n)},
        compiler_params=params(),
        name="after",
    )(*values, *earlier)


def combine(lefts, pieces, masks, final_shift, seqs):
    pairs, depth, _ = lefts[0].shape
    span = pieces[0].shape[0] * len(pieces)
    total = 2 * pairs * len(lefts)
    return pl.pallas_call(
        functools.partial(combine_kernel, seqs, masks, len(lefts)),
        out_shape=jax.ShapeDtypeStruct((total, span, LANES), BF16),
        in_specs=[VMEM] * (len(lefts) + len(pieces) + 1),
        out_specs=HBM,
        scratch_shapes=[
            pltpu.VMEM((span, depth), BF16),
            pltpu.VMEM((total // 2, 2, span, LANES), BF16),
            pltpu.SemaphoreType.DMA((total // 2,)),
        ],
        compiler_params=params(),
        cost_estimate=pl.CostEstimate(
            flops=2 * total * span * LANES * depth, bytes_accessed=total * span * LANES * 2, transcendentals=0
        ),
        name="combine",
    )(*[keep(left) for left in lefts], *pieces, final_shift[None])


def linear(target):
    moves = []
    for r in range(16):
        for c in range(2):
            t = target(r, c, r // 8 == c)
            if t is not None:
                moves.append((r * 2 + c, t[0] * 2 + t[1]))
    return moves


def flip(value, bits):
    return lax.ppermute(value, "row", [(r, r ^ bits) for r in range(16)])


def plain(x, gain, shift, first, first_shift, second, second_shift, final, final_shift):
    seqs, here, _ = x.shape
    width = first.shape[1]
    wide = x.astype(F32)
    centered = wide - jnp.mean(wide, axis=-1, keepdims=True)
    variance = jnp.mean(centered * centered, axis=-1, keepdims=True)
    normed = (centered * lax.rsqrt(variance + 1e-05) * gain + shift).astype(BF16)
    left = (jnp.einsum("src,ck->rsk", normed, first, preferred_element_type=F32) + first_shift).astype(BF16)
    right = (jnp.einsum("src,ck->rks", normed, second, preferred_element_type=F32) + second_shift).astype(BF16)
    right = right.reshape(here, width, seqs // RUN, RUN).transpose(0, 2, 1, 3).reshape(here, seqs * width)
    left = lax.all_gather(left.reshape(here, seqs * width), "col", axis=0, tiled=True)
    groups = LANES // width
    left = left.reshape(groups, -1, width).transpose(1, 0, 2).reshape(-1, LANES)
    every = lax.all_gather(right, ("row", "col"), axis=0, tiled=True)
    span = every.shape[0] // lax.axis_size("col")
    mine = lax.dynamic_slice_in_dim(every, lax.axis_index("col") * span, span, 0)
    spread_left, _ = spread(left, final, seqs, width)
    return combine([spread_left], [mine], (0,), final_shift, seqs)


def per_device(x, gain, shift, first, first_shift, second, second_shift, final, final_shift):
    seqs, here, _ = x.shape
    width = first.shape[1]
    if (lax.axis_size("row"), lax.axis_size("col"), here % 24) != (16, 2, 0):
        return plain(x, gain, shift, first, first_shift, second, second_shift, final, final_shift)
    right, left, final = project(x, gain, shift, first, first_shift, second, second_shift, final)
    both = ("row", "col")
    far = lax.ppermute(right, both, linear(lambda r, c, i: (r ^ 1, c) if i else (r ^ 8, 1 - c)))
    beside = lax.ppermute(left, "col", [(0, 1), (1, 0)])
    near = lax.ppermute(right, both, linear(lambda r, c, i: (r ^ 8, c) if i else (r, 1 - c)))
    own, pairs = spread(left, final, seqs, width)
    pair = arrange(right, near, far, pairs)
    gathered = [flip(pair, bits) for bits in (2, 4, 6)]
    lefts = [own, spread(beside, final, seqs, width, pairs)]
    pieces = [pair, *after(gathered, keep(lefts[1]))]
    pieces += [flip(piece, 1) for piece in pieces]
    return combine(lefts, pieces, (0, 2, 4, 6, 1, 3, 5, 7), final_shift, seqs)


def solution(mesh):
    return jax.shard_map(
        per_device,
        mesh=mesh,
        in_specs=(P("groups", ("row", "col"), None), P(), P(), P(), P(), P(), P(), P(), P()),
        out_specs=P(("groups", "row"), "col", None),
        check_vma=False,
    )
```

```python
import functools

import jax
import jax.numpy as jnp
from jax import lax
from jax.experimental import pallas as pl
from jax.experimental.pallas import tpu as pltpu
from jax.sharding import PartitionSpec as P

F32, BF16 = jnp.float32, jnp.bfloat16
LANES = 128
RUN = 8


def project_kernel(*refs):
    sources, (r_ref, l_ref, final_ref, held), buffers, sems = refs[:8], refs[8:12], refs[12:19], refs[19]
    targets = (*buffers, final_ref)
    copies = [pltpu.make_async_copy(src, dst, sems.at[k]) for k, (src, dst) in enumerate(zip(sources, targets))]
    for copy in copies:
        copy.start()
    for copy in copies[:-1]:
        copy.wait()
    x_ref, gain_ref, shift_ref, left_ref, left_shift_ref, right_ref, right_shift_ref = buffers
    seqs, here, channels = x_ref.shape
    width = left_ref.shape[0]
    groups = LANES // width
    x = x_ref[...].astype(F32).reshape(seqs * here, channels)
    centered = x - jnp.mean(x, axis=-1, keepdims=True)
    variance = jnp.mean(centered * centered, axis=-1, keepdims=True)
    normed = (centered * lax.rsqrt(variance + 1e-05) * gain_ref[...] + shift_ref[...]).astype(BF16)
    matrices = jnp.concatenate([left_ref[...]] * groups + [right_ref[...]] * groups, axis=0)
    shifts = jnp.concatenate([left_shift_ref[...]] * groups + [right_shift_ref[...]] * groups, axis=1)
    both = lax.dot_general(normed, matrices, (((1,), (1,)), ((), ())), preferred_element_type=F32) + shifts
    held[0], held[1] = both[:, :LANES], both[:, LANES:]
    group = lax.broadcasted_iota(jnp.int32, (1, LANES), 1) // width
    per = here // groups
    for i in range(per):
        packed = held[0, pl.ds(i, seqs, stride=here), :]
        for g in range(1, groups):
            packed = jnp.where(group == g, held[0, pl.ds(g * per + i, seqs, stride=here), :], packed)
        l_ref[i * seqs : (i + 1) * seqs, :] = packed.astype(BF16)
    rows = []
    for q in range(seqs // RUN):
        tiles = []
        for t in range(RUN // groups):
            s = q * RUN + t * groups
            packed = held[1, s * here : (s + 1) * here, :]
            for g in range(1, groups):
                packed = jnp.where(group == g, held[1, (s + g) * here : (s + g + 1) * here, :], packed)
            tiles.append(packed)
        rows.append(jnp.concatenate(tiles, axis=1))
    packed = jnp.concatenate(rows, axis=0).astype(BF16)
    span = RUN * width
    a = lax.broadcasted_iota(jnp.int32, (span, span), 0)
    b = lax.broadcasted_iota(jnp.int32, (span, span), 1)
    order = jnp.where((a % width) * RUN + a // width == b, 1.0, 0.0).astype(BF16)
    ordered = jnp.dot(packed, order, preferred_element_type=F32).astype(BF16)
    for q in range(seqs // RUN):
        r_ref[:, q * span : (q + 1) * span] = ordered[q * here : (q + 1) * here, :]
    copies[-1].wait()


def spread_left(seqs, width, l_ref, pairs, t_ref):
    groups = LANES // width
    residues = l_ref.shape[0] // seqs * groups
    left = jnp.concatenate([l_ref[:, g * width : (g + 1) * width] for g in range(groups)], axis=0)
    for m in range(width // 2):
        wide_out = jnp.dot(left, pairs[m], preferred_element_type=F32)
        for i in range(residues):
            for q in range(seqs // RUN):
                s = i * seqs + q * RUN
                block = jnp.concatenate([wide_out[s : s + RUN, :LANES], wide_out[s : s + RUN, LANES:]], axis=0)
                start = q * RUN * width + m * 2 * RUN
                t_ref[i // 2, start : start + 2 * RUN, (i % 2) * LANES : (i % 2 + 1) * LANES] = block.astype(BF16)


def spread_first_kernel(seqs, width, l_ref, f_ref, t_ref, pairs, wide):
    wide[...] = f_ref[...].astype(F32)
    for d in range(width):
        pairs[d // 2, :, (d % 2) * LANES : (d % 2 + 1) * LANES] = wide[pl.ds(d, width, stride=width), :].astype(BF16)
    spread_left(seqs, width, l_ref, pairs, t_ref)


def spread_second_kernel(seqs, width, l_ref, pairs, t_ref):
    spread_left(seqs, width, l_ref, pairs, t_ref)


def arrange_kernel(own_ref, near_ref, far_ref, _, pair_ref):
    row, col = lax.axis_index("row"), lax.axis_index("col")
    inside = row // 8 == col
    here = own_ref.shape[0]
    own, near, far = own_ref[...], near_ref[...], far_ref[...]
    same, other = jnp.where(inside, own, near), jnp.where(inside, near, far)
    pair_ref[:here, :] = jnp.where(col == 0, same, other)
    pair_ref[here:, :] = jnp.where(col == 0, other, same)


def order_kernel(*refs):
    pass


def combine_kernel(seqs, masks, n_left, last, *refs):
    lefts, pieces = refs[:n_left], refs[n_left : n_left + len(masks)]
    shift_ref, refs = refs[n_left + len(masks)], refs[n_left + len(masks) + 1 :]
    stage, right = refs[-3], refs[-2]
    rows = pieces[0].shape[0]
    pairs = lefts[0].shape[0]
    count = stage.shape[2] // rows
    spot = lax.rem(lax.axis_index("row"), count) if count > 1 else 0
    run = 2 * rows if count > 1 else rows
    for n, (mask, piece) in enumerate(zip(masks, pieces)):
        start = (n // 2 * 2 + jnp.bitwise_and(jnp.bitwise_xor(spot, mask), 1)) * rows if count > 1 else 0
        right[pl.ds(pl.multiple_of(start, rows), rows), :] = piece[...]
    shift = jnp.concatenate([shift_ref[...]] * 2, axis=1)
    unroll = next(u for u in (12, 6, 4, 3, 2, 1) if pairs % u == 0)
    places = [
        pl.multiple_of(jnp.bitwise_xor(spot, masks[n]) // 2 * run, run) if count > 1 else 0
        for n in range(0, len(masks), 2)
    ]

    for h, left in enumerate(lefts):
        first = 2 * pairs * (jnp.bitwise_xor(lax.axis_index("col"), h) if n_left > 1 else 0)

        def step(n, carry, left=left, first=first, h=h):
            for u in range(unroll):
                p = n * unroll + u
                update = jnp.dot(right[...], left[p], preferred_element_type=F32) * (1.0 / seqs) + shift
                for k, place in enumerate(places):
                    block = update[k * run : (k + 1) * run].astype(BF16)
                    stage[h * pairs + p, 0, pl.ds(place, run)] = block[:, :LANES]
                    stage[h * pairs + p, 1, pl.ds(place, run)] = block[:, LANES:]
                if last:
                    out_ref, sem = refs[-4], refs[-1]
                    pltpu.make_async_copy(stage.at[h * pairs + p], out_ref.at[pl.ds(first + 2 * p, 2)], sem).start()
            return carry

        lax.fori_loop(0, pairs // unroll, step, 0)
    if last:
        out_ref, sem = refs[-4], refs[-1]
        pltpu.make_async_copy(out_ref, out_ref, sem).wait()


VMEM = pl.BlockSpec(memory_space=pltpu.VMEM)
HBM = pl.BlockSpec(memory_space=pltpu.HBM)


def params():
    return pltpu.CompilerParams(vmem_limit_bytes=12 << 20)


def keep(value):
    return pltpu.with_memory_space_constraint(value, pltpu.VMEM)


def project(x, gain, shift, first, first_shift, second, second_shift, final):
    seqs, here, channels = x.shape
    width = first.shape[1]
    args = (x, gain[None], shift[None], first.T, first_shift[None], second.T, second_shift[None], final)
    args = [pltpu.with_memory_space_constraint(a, pltpu.HBM) for a in args]
    return pl.pallas_call(
        project_kernel,
        out_shape=(
            jax.ShapeDtypeStruct((here, seqs * width), BF16),
            jax.ShapeDtypeStruct((here * width // LANES * seqs, LANES), BF16),
            pltpu.VMEM(final.shape, BF16),
        ),
        in_specs=[HBM] * len(args),
        out_specs=(VMEM, VMEM, VMEM),
        scratch_shapes=[pltpu.VMEM((2, seqs * here, LANES), F32)]
        + [pltpu.VMEM(a.shape, a.dtype) for a in args[:-1]]
        + [pltpu.SemaphoreType.DMA((len(args),))],
        compiler_params=params(),
        cost_estimate=pl.CostEstimate(flops=2 * x.size * 256, bytes_accessed=2 * x.size, transcendentals=0),
        name="project",
    )(*args)


def spread(left, final, seqs, width, pairs=None):
    residues = left.shape[0] // seqs * (LANES // width)
    wide = pltpu.VMEM((residues // 2, seqs * width, 2 * LANES), BF16)
    cost = pl.CostEstimate(
        flops=2 * residues * seqs * 256 * width * LANES, bytes_accessed=left.size * 2, transcendentals=0
    )
    if pairs is None:
        return pl.pallas_call(
            functools.partial(spread_first_kernel, seqs, width),
            out_shape=(wide, pltpu.VMEM((width // 2, width, 2 * LANES), BF16)),
            in_specs=[VMEM] * 2,
            out_specs=(VMEM, VMEM),
            scratch_shapes=[pltpu.VMEM(final.shape, F32)],
            compiler_params=params(),
            cost_estimate=cost,
            name="spread_first",
        )(left, keep(final))
    return pl.pallas_call(
        functools.partial(spread_second_kernel, seqs, width),
        out_shape=wide,
        in_specs=[VMEM] * 2,
        out_specs=VMEM,
        compiler_params=params(),
        cost_estimate=cost,
        name="spread_second",
    )(left, keep(pairs))


def arrange(own, near, far, after):
    return pl.pallas_call(
        arrange_kernel,
        out_shape=jax.ShapeDtypeStruct((2 * own.shape[0], own.shape[1]), BF16),
        in_specs=[VMEM] * 4,
        out_specs=VMEM,
        compiler_params=params(),
        name="arrange",
    )(own, near, far, keep(after))


def after(values, *earlier):
    n = len(values)
    return pl.pallas_call(
        order_kernel,
        out_shape=[jax.ShapeDtypeStruct(v.shape, v.dtype) for v in values],
        in_specs=[pl.BlockSpec(memory_space=pl.ANY)] * (n + len(earlier)),
        out_specs=[pl.BlockSpec(memory_space=pl.ANY)] * n,
        input_output_aliases={k: k for k in range(n)},
        compiler_params=params(),
        name="after",
    )(*values, *earlier)


def combine(lefts, pieces, masks, final_shift, seqs, span, begun=None, last=True):
    pairs, depth, _ = lefts[0].shape
    rows = pieces[0].shape[0] * len(pieces)
    total = 2 * pairs * len(lefts)
    stage = pltpu.VMEM((total // 2, 2, span, LANES), BF16)
    args = [*[keep(left) for left in lefts], *pieces, final_shift[None]] + ([] if begun is None else [keep(begun)])
    outs = ([jax.ShapeDtypeStruct((total, span, LANES), BF16)] if last else []) + [stage]
    return pl.pallas_call(
        functools.partial(combine_kernel, seqs, masks, len(lefts), last),
        out_shape=outs,
        in_specs=[VMEM] * len(args),
        out_specs=[HBM, VMEM] if last else [VMEM],
        input_output_aliases={} if begun is None else {len(args) - 1: len(outs) - 1},
        scratch_shapes=[pltpu.VMEM((rows, depth), BF16), pltpu.SemaphoreType.DMA],
        compiler_params=params(),
        cost_estimate=pl.CostEstimate(
            flops=2 * total * rows * LANES * depth, bytes_accessed=total * rows * LANES * 2, transcendentals=0
        ),
        name="combine_last" if last else "combine_some",
    )(*args)[0]


def linear(target):
    moves = []
    for r in range(16):
        for c in range(2):
            t = target(r, c, r // 8 == c)
            if t is not None:
                moves.append((r * 2 + c, t[0] * 2 + t[1]))
    return moves


def flip(value, bits):
    return lax.ppermute(value, "row", [(r, r ^ bits) for r in range(16)])


def plain(x, gain, shift, first, first_shift, second, second_shift, final, final_shift):
    seqs, here, _ = x.shape
    width = first.shape[1]
    wide = x.astype(F32)
    centered = wide - jnp.mean(wide, axis=-1, keepdims=True)
    variance = jnp.mean(centered * centered, axis=-1, keepdims=True)
    normed = (centered * lax.rsqrt(variance + 1e-05) * gain + shift).astype(BF16)
    left = (jnp.einsum("src,ck->rsk", normed, first, preferred_element_type=F32) + first_shift).astype(BF16)
    right = (jnp.einsum("src,ck->rks", normed, second, preferred_element_type=F32) + second_shift).astype(BF16)
    right = right.reshape(here, width, seqs // RUN, RUN).transpose(0, 2, 1, 3).reshape(here, seqs * width)
    left = lax.all_gather(left.reshape(here, seqs * width), "col", axis=0, tiled=True)
    groups = LANES // width
    left = left.reshape(groups, -1, width).transpose(1, 0, 2).reshape(-1, LANES)
    every = lax.all_gather(right, ("row", "col"), axis=0, tiled=True)
    span = every.shape[0] // lax.axis_size("col")
    mine = lax.dynamic_slice_in_dim(every, lax.axis_index("col") * span, span, 0)
    spread_left, _ = spread(left, final, seqs, width)
    return combine([spread_left], [mine], (0,), final_shift, seqs, span)


def per_device(x, gain, shift, first, first_shift, second, second_shift, final, final_shift):
    seqs, here, _ = x.shape
    width = first.shape[1]
    if (lax.axis_size("row"), lax.axis_size("col"), here % 24) != (16, 2, 0):
        return plain(x, gain, shift, first, first_shift, second, second_shift, final, final_shift)
    right, left, final = project(x, gain, shift, first, first_shift, second, second_shift, final)
    both = ("row", "col")
    far = lax.ppermute(right, both, linear(lambda r, c, i: (r ^ 1, c) if i else (r ^ 8, 1 - c)))
    beside = lax.ppermute(left, "col", [(0, 1), (1, 0)])
    near = lax.ppermute(right, both, linear(lambda r, c, i: (r ^ 8, c) if i else (r, 1 - c)))
    own, pairs = spread(left, final, seqs, width)
    pair = arrange(right, near, far, pairs)
    first, second, third = [flip(pair, bits) for bits in (2, 4, 6)]
    lefts = [own, spread(beside, final, seqs, width, pairs)]
    span = 16 * here
    begun = combine(lefts, [pair, flip(pair, 1)], (0, 1), final_shift, seqs, span, last=False)
    first, second, third = [after([piece], keep(begun))[0] for piece in (first, second, third)]
    pieces = [first, flip(first, 1), second, flip(second, 1), third, flip(third, 1)]
    return combine(lefts, pieces, (2, 3, 4, 5, 6, 7), final_shift, seqs, span, begun)


def solution(mesh):
    return jax.shard_map(
        per_device,
        mesh=mesh,
        in_specs=(P("groups", ("row", "col"), None), P(), P(), P(), P(), P(), P(), P(), P()),
        out_specs=P(("groups", "row"), "col", None),
        check_vma=False,
    )
```

```python
import functools

import jax
import jax.numpy as jnp
from jax import lax
from jax.experimental import pallas as pl
from jax.experimental.pallas import tpu as pltpu
from jax.sharding import PartitionSpec as P

F32, BF16 = jnp.float32, jnp.bfloat16
LANES = 128
RUN = 8


def project_kernel(*refs):
    sources, (r_ref, l_ref, final_ref, held), buffers, sems = refs[:8], refs[8:12], refs[12:19], refs[19]
    targets = (*buffers, final_ref)
    copies = [pltpu.make_async_copy(src, dst, sems.at[k]) for k, (src, dst) in enumerate(zip(sources, targets))]
    for copy in copies:
        copy.start()
    for copy in copies[:-1]:
        copy.wait()
    x_ref, gain_ref, shift_ref, left_ref, left_shift_ref, right_ref, right_shift_ref = buffers
    seqs, here, channels = x_ref.shape
    width = left_ref.shape[0]
    groups = LANES // width
    x = x_ref[...].astype(F32).reshape(seqs * here, channels)
    centered = x - jnp.mean(x, axis=-1, keepdims=True)
    variance = jnp.mean(centered * centered, axis=-1, keepdims=True)
    normed = (centered * lax.rsqrt(variance + 1e-05) * gain_ref[...] + shift_ref[...]).astype(BF16)
    matrices = jnp.concatenate([left_ref[...]] * groups + [right_ref[...]] * groups, axis=0)
    shifts = jnp.concatenate([left_shift_ref[...]] * groups + [right_shift_ref[...]] * groups, axis=1)
    both = lax.dot_general(normed, matrices, (((1,), (1,)), ((), ())), preferred_element_type=F32) + shifts
    held[0], held[1] = both[:, :LANES], both[:, LANES:]
    group = lax.broadcasted_iota(jnp.int32, (1, LANES), 1) // width
    per = here // groups
    for i in range(per):
        packed = held[0, pl.ds(i, seqs, stride=here), :]
        for g in range(1, groups):
            packed = jnp.where(group == g, held[0, pl.ds(g * per + i, seqs, stride=here), :], packed)
        l_ref[i * seqs : (i + 1) * seqs, :] = packed.astype(BF16)
    rows = []
    for q in range(seqs // RUN):
        tiles = []
        for t in range(RUN // groups):
            s = q * RUN + t * groups
            packed = held[1, s * here : (s + 1) * here, :]
            for g in range(1, groups):
                packed = jnp.where(group == g, held[1, (s + g) * here : (s + g + 1) * here, :], packed)
            tiles.append(packed)
        rows.append(jnp.concatenate(tiles, axis=1))
    packed = jnp.concatenate(rows, axis=0).astype(BF16)
    span = RUN * width
    a = lax.broadcasted_iota(jnp.int32, (span, span), 0)
    b = lax.broadcasted_iota(jnp.int32, (span, span), 1)
    order = jnp.where((a % width) * RUN + a // width == b, 1.0, 0.0).astype(BF16)
    ordered = jnp.dot(packed, order, preferred_element_type=F32).astype(BF16)
    for q in range(seqs // RUN):
        r_ref[:, q * span : (q + 1) * span] = ordered[q * here : (q + 1) * here, :]
    copies[-1].wait()


def spread_left(seqs, width, l_ref, pairs, t_ref):
    groups = LANES // width
    residues = l_ref.shape[0] // seqs * groups
    left = jnp.concatenate([l_ref[:, g * width : (g + 1) * width] for g in range(groups)], axis=0)
    for m in range(width // 2):
        wide_out = jnp.dot(left, pairs[m], preferred_element_type=F32)
        for i in range(residues):
            for q in range(seqs // RUN):
                s = i * seqs + q * RUN
                block = jnp.concatenate([wide_out[s : s + RUN, :LANES], wide_out[s : s + RUN, LANES:]], axis=0)
                start = q * RUN * width + m * 2 * RUN
                t_ref[i // 2, start : start + 2 * RUN, (i % 2) * LANES : (i % 2 + 1) * LANES] = block.astype(BF16)


def spread_first_kernel(seqs, width, l_ref, f_ref, t_ref, pairs, wide):
    wide[...] = f_ref[...].astype(F32)
    for d in range(width):
        pairs[d // 2, :, (d % 2) * LANES : (d % 2 + 1) * LANES] = wide[pl.ds(d, width, stride=width), :].astype(BF16)
    spread_left(seqs, width, l_ref, pairs, t_ref)


def spread_second_kernel(seqs, width, l_ref, pairs, t_ref):
    spread_left(seqs, width, l_ref, pairs, t_ref)


def arrange_kernel(own_ref, near_ref, far_ref, _, pair_ref):
    row, col = lax.axis_index("row"), lax.axis_index("col")
    inside = row // 8 == col
    here = own_ref.shape[0]
    own, near, far = own_ref[...], near_ref[...], far_ref[...]
    same, other = jnp.where(inside, own, near), jnp.where(inside, near, far)
    pair_ref[:here, :] = jnp.where(col == 0, same, other)
    pair_ref[here:, :] = jnp.where(col == 0, other, same)


def order_kernel(*refs):
    pass


def combine_kernel(seqs, masks, n_left, offset, last, skip, *refs):
    refs = refs[skip:]
    shift_ref, *refs = refs
    lefts, pieces = refs[:n_left], refs[n_left : n_left + len(masks)]
    stage, right = refs[-3], refs[-2]
    rows = pieces[0].shape[0]
    pairs = lefts[0].shape[0]
    count = stage.shape[2] // rows
    spot = lax.rem(lax.axis_index("row"), count) if count > 1 else 0
    run = 2 * rows if count > 1 else rows
    for n, (mask, piece) in enumerate(zip(masks, pieces)):
        start = (n // 2 * 2 + jnp.bitwise_and(jnp.bitwise_xor(spot, mask), 1)) * rows if count > 1 else 0
        right[pl.ds(pl.multiple_of(start, rows), rows), :] = piece[...]
    shift = jnp.concatenate([shift_ref[...]] * 2, axis=1)
    unroll = next(u for u in (12, 6, 4, 3, 2, 1) if pairs % u == 0)
    places = [
        pl.multiple_of(jnp.bitwise_xor(spot, masks[n]) // 2 * run, run) if count > 1 else 0
        for n in range(0, len(masks), 2)
    ]

    for h, left in enumerate(lefts):
        first = 2 * pairs * (jnp.bitwise_xor(lax.axis_index("col"), h) if n_left > 1 else 0)

        def step(n, carry, left=left, first=first, h=h):
            for u in range(unroll):
                p = n * unroll + u
                update = jnp.dot(right[...], left[p], preferred_element_type=F32) * (1.0 / seqs) + shift
                for k, place in enumerate(places):
                    block = update[k * run : (k + 1) * run].astype(BF16)
                    stage[offset + h * pairs + p, 0, pl.ds(place, run)] = block[:, :LANES]
                    stage[offset + h * pairs + p, 1, pl.ds(place, run)] = block[:, LANES:]
                if last:
                    out_ref, sem = refs[-4], refs[-1]
                    pltpu.make_async_copy(stage.at[h * pairs + p], out_ref.at[pl.ds(first + 2 * p, 2)], sem).start()
            return carry

        lax.fori_loop(0, pairs // unroll, step, 0)
    if last:
        out_ref, sem = refs[-4], refs[-1]
        pltpu.make_async_copy(out_ref, out_ref, sem).wait()


VMEM = pl.BlockSpec(memory_space=pltpu.VMEM)
HBM = pl.BlockSpec(memory_space=pltpu.HBM)


def params():
    return pltpu.CompilerParams(vmem_limit_bytes=12 << 20)


def keep(value):
    return pltpu.with_memory_space_constraint(value, pltpu.VMEM)


def project(x, gain, shift, first, first_shift, second, second_shift, final):
    seqs, here, channels = x.shape
    width = first.shape[1]
    args = (x, gain[None], shift[None], first.T, first_shift[None], second.T, second_shift[None], final)
    args = [pltpu.with_memory_space_constraint(a, pltpu.HBM) for a in args]
    return pl.pallas_call(
        project_kernel,
        out_shape=(
            jax.ShapeDtypeStruct((here, seqs * width), BF16),
            jax.ShapeDtypeStruct((here * width // LANES * seqs, LANES), BF16),
            pltpu.VMEM(final.shape, BF16),
        ),
        in_specs=[HBM] * len(args),
        out_specs=(VMEM, VMEM, VMEM),
        scratch_shapes=[pltpu.VMEM((2, seqs * here, LANES), F32)]
        + [pltpu.VMEM(a.shape, a.dtype) for a in args[:-1]]
        + [pltpu.SemaphoreType.DMA((len(args),))],
        compiler_params=params(),
        cost_estimate=pl.CostEstimate(flops=2 * x.size * 256, bytes_accessed=2 * x.size, transcendentals=0),
        name="project",
    )(*args)


def spread(left, final, seqs, width, pairs=None):
    residues = left.shape[0] // seqs * (LANES // width)
    wide = pltpu.VMEM((residues // 2, seqs * width, 2 * LANES), BF16)
    cost = pl.CostEstimate(
        flops=2 * residues * seqs * 256 * width * LANES, bytes_accessed=left.size * 2, transcendentals=0
    )
    if pairs is None:
        return pl.pallas_call(
            functools.partial(spread_first_kernel, seqs, width),
            out_shape=(wide, pltpu.VMEM((width // 2, width, 2 * LANES), BF16)),
            in_specs=[VMEM] * 2,
            out_specs=(VMEM, VMEM),
            scratch_shapes=[pltpu.VMEM(final.shape, F32)],
            compiler_params=params(),
            cost_estimate=cost,
            name="spread_first",
        )(left, keep(final))
    return pl.pallas_call(
        functools.partial(spread_second_kernel, seqs, width),
        out_shape=wide,
        in_specs=[VMEM] * 2,
        out_specs=VMEM,
        compiler_params=params(),
        cost_estimate=cost,
        name="spread_second",
    )(left, keep(pairs))


def arrange(own, near, far, after):
    return pl.pallas_call(
        arrange_kernel,
        out_shape=jax.ShapeDtypeStruct((2 * own.shape[0], own.shape[1]), BF16),
        in_specs=[VMEM] * 4,
        out_specs=VMEM,
        compiler_params=params(),
        name="arrange",
    )(own, near, far, keep(after))


def after(values, *earlier):
    n = len(values)
    return pl.pallas_call(
        order_kernel,
        out_shape=[jax.ShapeDtypeStruct(v.shape, v.dtype) for v in values],
        in_specs=[pl.BlockSpec(memory_space=pl.ANY)] * (n + len(earlier)),
        out_specs=[pl.BlockSpec(memory_space=pl.ANY)] * n,
        input_output_aliases={k: k for k in range(n)},
        compiler_params=params(),
        name="after",
    )(*values, *earlier)


def combine(lefts, pieces, masks, final_shift, seqs, span, begun=None, offset=0, total=None, follow=()):
    last = total is None
    pairs, depth, _ = lefts[0].shape
    rows = pieces[0].shape[0] * len(pieces)
    total = total or 2 * pairs * len(lefts)
    stage = pltpu.VMEM((total // 2, 2, span, LANES), BF16)
    first = ([] if begun is None else [keep(begun)]) + [*follow]
    args = [*first, final_shift[None], *[keep(left) for left in lefts], *pieces]
    outs = ([jax.ShapeDtypeStruct((total, span, LANES), BF16)] if last else []) + [stage]
    return pl.pallas_call(
        functools.partial(combine_kernel, seqs, masks, len(lefts), offset, last, len(first)),
        out_shape=outs,
        in_specs=[VMEM] * len(args),
        out_specs=[HBM, VMEM] if last else [VMEM],
        input_output_aliases={} if begun is None else {0: len(outs) - 1},
        scratch_shapes=[pltpu.VMEM((rows, depth), BF16), pltpu.SemaphoreType.DMA],
        compiler_params=params(),
        cost_estimate=pl.CostEstimate(
            flops=4 * pairs * len(lefts) * rows * LANES * depth, bytes_accessed=0, transcendentals=0
        ),
        name="combine_last" if last else "combine_some",
    )(*args)[0]


def linear(target):
    moves = []
    for r in range(16):
        for c in range(2):
            t = target(r, c, r // 8 == c)
            if t is not None:
                moves.append((r * 2 + c, t[0] * 2 + t[1]))
    return moves


def flip(value, bits):
    return lax.ppermute(value, "row", [(r, r ^ bits) for r in range(16)])


def plain(x, gain, shift, first, first_shift, second, second_shift, final, final_shift):
    seqs, here, _ = x.shape
    width = first.shape[1]
    wide = x.astype(F32)
    centered = wide - jnp.mean(wide, axis=-1, keepdims=True)
    variance = jnp.mean(centered * centered, axis=-1, keepdims=True)
    normed = (centered * lax.rsqrt(variance + 1e-05) * gain + shift).astype(BF16)
    left = (jnp.einsum("src,ck->rsk", normed, first, preferred_element_type=F32) + first_shift).astype(BF16)
    right = (jnp.einsum("src,ck->rks", normed, second, preferred_element_type=F32) + second_shift).astype(BF16)
    right = right.reshape(here, width, seqs // RUN, RUN).transpose(0, 2, 1, 3).reshape(here, seqs * width)
    left = lax.all_gather(left.reshape(here, seqs * width), "col", axis=0, tiled=True)
    groups = LANES // width
    left = left.reshape(groups, -1, width).transpose(1, 0, 2).reshape(-1, LANES)
    every = lax.all_gather(right, ("row", "col"), axis=0, tiled=True)
    span = every.shape[0] // lax.axis_size("col")
    mine = lax.dynamic_slice_in_dim(every, lax.axis_index("col") * span, span, 0)
    spread_left, _ = spread(left, final, seqs, width)
    return combine([spread_left], [mine], (0,), final_shift, seqs, span)


def per_device(x, gain, shift, first, first_shift, second, second_shift, final, final_shift):
    seqs, here, _ = x.shape
    width = first.shape[1]
    if (lax.axis_size("row"), lax.axis_size("col"), here % 24) != (16, 2, 0):
        return plain(x, gain, shift, first, first_shift, second, second_shift, final, final_shift)
    right, left, final = project(x, gain, shift, first, first_shift, second, second_shift, final)
    both = ("row", "col")
    far = lax.ppermute(right, both, linear(lambda r, c, i: (r ^ 1, c) if i else (r ^ 8, 1 - c)))
    near = lax.ppermute(right, both, linear(lambda r, c, i: (r ^ 8, c) if i else (r, 1 - c)))
    own, pairs = spread(left, final, seqs, width)
    beside = lax.ppermute(after([left], keep(pairs))[0], "col", [(0, 1), (1, 0)])
    pair = arrange(right, near, far, pairs)
    first, second, third = [flip(pair, bits) for bits in (2, 4, 6)]
    lefts = [own, spread(beside, final, seqs, width, pairs)]
    span = 16 * here
    some, masks, total = [pair, flip(pair, 1)], (0, 1), 2 * here
    begun = combine(lefts[:1], some, masks, final_shift, seqs, span, None, 0, total)
    first, second, third = after([first, second, third], keep(begun), keep(lefts[1]))
    begun = combine(lefts[1:], some, masks, final_shift, seqs, span, begun, here // 2, total, [first])
    pieces = [first, flip(first, 1), second, flip(second, 1), third, flip(third, 1)]
    return combine(lefts, pieces, (2, 3, 4, 5, 6, 7), final_shift, seqs, span, begun)


def solution(mesh):
    return jax.shard_map(
        per_device,
        mesh=mesh,
        in_specs=(P("groups", ("row", "col"), None), P(), P(), P(), P(), P(), P(), P(), P()),
        out_specs=P(("groups", "row"), "col", None),
        check_vma=False,
    )
```

```python
import functools

import jax
import jax.numpy as jnp
from jax import lax
from jax.experimental import pallas as pl
from jax.experimental.pallas import tpu as pltpu
from jax.sharding import PartitionSpec as P

F32, BF16 = jnp.float32, jnp.bfloat16
LANES = 128
RUN = 8


def project_kernel(*refs):
    sources, (r_ref, l_ref, final_ref, held), buffers, sems = refs[:8], refs[8:12], refs[12:19], refs[19]
    targets = (*buffers, final_ref)
    copies = [pltpu.make_async_copy(src, dst, sems.at[k]) for k, (src, dst) in enumerate(zip(sources, targets))]
    for copy in copies:
        copy.start()
    for copy in copies[:-1]:
        copy.wait()
    x_ref, gain_ref, shift_ref, left_ref, left_shift_ref, right_ref, right_shift_ref = buffers
    seqs, here, channels = x_ref.shape
    width = left_ref.shape[0]
    groups = LANES // width
    x = x_ref[...].astype(F32).reshape(seqs * here, channels)
    centered = x - jnp.mean(x, axis=-1, keepdims=True)
    variance = jnp.mean(centered * centered, axis=-1, keepdims=True)
    normed = (centered * lax.rsqrt(variance + 1e-05) * gain_ref[...] + shift_ref[...]).astype(BF16)
    matrices = jnp.concatenate([left_ref[...]] * groups + [right_ref[...]] * groups, axis=0)
    shifts = jnp.concatenate([left_shift_ref[...]] * groups + [right_shift_ref[...]] * groups, axis=1)
    both = lax.dot_general(normed, matrices, (((1,), (1,)), ((), ())), preferred_element_type=F32) + shifts
    held[0], held[1] = both[:, :LANES], both[:, LANES:]
    group = lax.broadcasted_iota(jnp.int32, (1, LANES), 1) // width
    per = here // groups
    for i in range(per):
        packed = held[0, pl.ds(i, seqs, stride=here), :]
        for g in range(1, groups):
            packed = jnp.where(group == g, held[0, pl.ds(g * per + i, seqs, stride=here), :], packed)
        l_ref[i * seqs : (i + 1) * seqs, :] = packed.astype(BF16)
    rows = []
    for q in range(seqs // RUN):
        tiles = []
        for t in range(RUN // groups):
            s = q * RUN + t * groups
            packed = held[1, s * here : (s + 1) * here, :]
            for g in range(1, groups):
                packed = jnp.where(group == g, held[1, (s + g) * here : (s + g + 1) * here, :], packed)
            tiles.append(packed)
        rows.append(jnp.concatenate(tiles, axis=1))
    packed = jnp.concatenate(rows, axis=0).astype(BF16)
    span = RUN * width
    a = lax.broadcasted_iota(jnp.int32, (span, span), 0)
    b = lax.broadcasted_iota(jnp.int32, (span, span), 1)
    order = jnp.where((a % width) * RUN + a // width == b, 1.0, 0.0).astype(BF16)
    ordered = jnp.dot(packed, order, preferred_element_type=F32).astype(BF16)
    for q in range(seqs // RUN):
        r_ref[:, q * span : (q + 1) * span] = ordered[q * here : (q + 1) * here, :]
    copies[-1].wait()


def spread_left(seqs, width, l_ref, pairs, t_ref):
    groups = LANES // width
    residues = l_ref.shape[0] // seqs * groups
    left = jnp.concatenate([l_ref[:, g * width : (g + 1) * width] for g in range(groups)], axis=0)
    for m in range(width // 2):
        wide_out = jnp.dot(left, pairs[m], preferred_element_type=F32)
        for i in range(residues):
            for q in range(seqs // RUN):
                s = i * seqs + q * RUN
                block = jnp.concatenate([wide_out[s : s + RUN, :LANES], wide_out[s : s + RUN, LANES:]], axis=0)
                start = q * RUN * width + m * 2 * RUN
                t_ref[i // 2, start : start + 2 * RUN, (i % 2) * LANES : (i % 2 + 1) * LANES] = block.astype(BF16)


def spread_first_kernel(seqs, width, l_ref, f_ref, t_ref, pairs, wide):
    wide[...] = f_ref[...].astype(F32)
    for d in range(width):
        pairs[d // 2, :, (d % 2) * LANES : (d % 2 + 1) * LANES] = wide[pl.ds(d, width, stride=width), :].astype(BF16)
    spread_left(seqs, width, l_ref, pairs, t_ref)


def spread_second_kernel(seqs, width, l_ref, pairs, t_ref):
    spread_left(seqs, width, l_ref, pairs, t_ref)


def arrange_kernel(own_ref, near_ref, far_ref, _, pair_ref):
    row, col = lax.axis_index("row"), lax.axis_index("col")
    inside = row // 8 == col
    here = own_ref.shape[0]
    own, near, far = own_ref[...], near_ref[...], far_ref[...]
    same, other = jnp.where(inside, own, near), jnp.where(inside, near, far)
    pair_ref[:here, :] = jnp.where(col == 0, same, other)
    pair_ref[here:, :] = jnp.where(col == 0, other, same)


def order_kernel(*refs):
    pass


def combine_kernel(seqs, masks, counts, offset, last, begun, *refs):
    refs = refs[begun:]
    lefts, pieces = refs[1 : 1 + len(counts)], refs[1 + len(counts) : 1 + len(counts) + len(masks)]
    shift_ref, stage, right = refs[0], refs[-3], refs[-2]
    rows = pieces[0].shape[0]
    pairs = lefts[0].shape[0]
    spots = stage.shape[2] // rows
    spot = lax.rem(lax.axis_index("row"), spots) if spots > 1 else 0
    places = [pl.multiple_of(jnp.bitwise_xor(spot, mask) * rows, rows) if spots > 1 else 0 for mask in masks]
    for n, piece in enumerate(pieces):
        right[n * rows : (n + 1) * rows, :] = piece[...]
    shift = jnp.concatenate([shift_ref[...]] * 2, axis=1)
    unroll = next(u for u in (12, 6, 4, 3, 2, 1) if pairs % u == 0)

    for h, (left, count) in enumerate(zip(lefts, counts)):
        first = 2 * pairs * (jnp.bitwise_xor(lax.axis_index("col"), h) if len(lefts) > 1 else 0)

        def step(n, carry, left=left, first=first, count=count, h=h):
            for u in range(unroll):
                p = n * unroll + u
                update = jnp.dot(right[: count * rows, :], left[p], preferred_element_type=F32) * (1.0 / seqs) + shift
                for k, place in enumerate(places[:count]):
                    block = update[k * rows : (k + 1) * rows].astype(BF16)
                    stage[offset + h * pairs + p, 0, pl.ds(place, rows)] = block[:, :LANES]
                    stage[offset + h * pairs + p, 1, pl.ds(place, rows)] = block[:, LANES:]
                if last:
                    out_ref, sem = refs[-4], refs[-1]
                    pltpu.make_async_copy(stage.at[h * pairs + p], out_ref.at[pl.ds(first + 2 * p, 2)], sem).start()
            return carry

        lax.fori_loop(0, pairs // unroll, step, 0)
    if last:
        out_ref, sem = refs[-4], refs[-1]
        pltpu.make_async_copy(out_ref, out_ref, sem).wait()


VMEM = pl.BlockSpec(memory_space=pltpu.VMEM)
HBM = pl.BlockSpec(memory_space=pltpu.HBM)


def params():
    return pltpu.CompilerParams(vmem_limit_bytes=12 << 20)


def keep(value):
    return pltpu.with_memory_space_constraint(value, pltpu.VMEM)


def project(x, gain, shift, first, first_shift, second, second_shift, final):
    seqs, here, channels = x.shape
    width = first.shape[1]
    args = (x, gain[None], shift[None], first.T, first_shift[None], second.T, second_shift[None], final)
    args = [pltpu.with_memory_space_constraint(a, pltpu.HBM) for a in args]
    return pl.pallas_call(
        project_kernel,
        out_shape=(
            jax.ShapeDtypeStruct((here, seqs * width), BF16),
            jax.ShapeDtypeStruct((here * width // LANES * seqs, LANES), BF16),
            pltpu.VMEM(final.shape, BF16),
        ),
        in_specs=[HBM] * len(args),
        out_specs=(VMEM, VMEM, VMEM),
        scratch_shapes=[pltpu.VMEM((2, seqs * here, LANES), F32)]
        + [pltpu.VMEM(a.shape, a.dtype) for a in args[:-1]]
        + [pltpu.SemaphoreType.DMA((len(args),))],
        compiler_params=params(),
        cost_estimate=pl.CostEstimate(flops=2 * x.size * 256, bytes_accessed=2 * x.size, transcendentals=0),
        name="project",
    )(*args)


def spread(left, final, seqs, width, pairs=None):
    residues = left.shape[0] // seqs * (LANES // width)
    wide = pltpu.VMEM((residues // 2, seqs * width, 2 * LANES), BF16)
    cost = pl.CostEstimate(
        flops=2 * residues * seqs * 256 * width * LANES, bytes_accessed=left.size * 2, transcendentals=0
    )
    if pairs is None:
        return pl.pallas_call(
            functools.partial(spread_first_kernel, seqs, width),
            out_shape=(wide, pltpu.VMEM((width // 2, width, 2 * LANES), BF16)),
            in_specs=[VMEM] * 2,
            out_specs=(VMEM, VMEM),
            scratch_shapes=[pltpu.VMEM(final.shape, F32)],
            compiler_params=params(),
            cost_estimate=cost,
            name="spread_first",
        )(left, final)
    return pl.pallas_call(
        functools.partial(spread_second_kernel, seqs, width),
        out_shape=wide,
        in_specs=[VMEM] * 2,
        out_specs=VMEM,
        compiler_params=params(),
        cost_estimate=cost,
        name="spread_second",
    )(left, keep(pairs))


def arrange(own, near, far, after):
    return pl.pallas_call(
        arrange_kernel,
        out_shape=jax.ShapeDtypeStruct((2 * own.shape[0], own.shape[1]), BF16),
        in_specs=[VMEM] * 4,
        out_specs=VMEM,
        compiler_params=params(),
        name="arrange",
    )(own, near, far, keep(after))


def after(values, *earlier):
    n = len(values)
    return pl.pallas_call(
        order_kernel,
        out_shape=[jax.ShapeDtypeStruct(v.shape, v.dtype) for v in values],
        in_specs=[pl.BlockSpec(memory_space=pl.ANY)] * (n + len(earlier)),
        out_specs=[pl.BlockSpec(memory_space=pl.ANY)] * n,
        input_output_aliases={k: k for k in range(n)},
        compiler_params=params(),
        name="after",
    )(*values, *earlier)


def combine(lefts, pieces, masks, counts, final_shift, seqs, span, begun=None, offset=0, total=None):
    last = total is None
    pairs, depth, _ = lefts[0].shape
    rows = pieces[0].shape[0]
    total = total or 2 * pairs * len(lefts)
    stage = pltpu.VMEM((total // 2, 2, span, LANES), BF16)
    args = [] if begun is None else [keep(begun)]
    args += [final_shift[None], *[keep(left) for left in lefts], *pieces]
    outs = ([jax.ShapeDtypeStruct((total, span, LANES), BF16)] if last else []) + [stage]
    return pl.pallas_call(
        functools.partial(combine_kernel, seqs, masks, counts, offset, last, 0 if begun is None else 1),
        out_shape=outs,
        in_specs=[VMEM] * len(args),
        out_specs=[HBM, VMEM] if last else [VMEM],
        input_output_aliases={} if begun is None else {0: len(outs) - 1},
        scratch_shapes=[pltpu.VMEM((rows * len(pieces), depth), BF16), pltpu.SemaphoreType.DMA],
        compiler_params=params(),
        cost_estimate=pl.CostEstimate(
            flops=4 * pairs * sum(counts) * rows * LANES * depth, bytes_accessed=0, transcendentals=0
        ),
        name="combine_last" if last else "combine_some",
    )(*args)[0]


def linear(target):
    moves = []
    for r in range(16):
        for c in range(2):
            t = target(r, c, r // 8 == c)
            if t is not None:
                moves.append((r * 2 + c, t[0] * 2 + t[1]))
    return moves


def flip(value, bits):
    return lax.ppermute(value, "row", [(r, r ^ bits) for r in range(16)])


def plain(x, gain, shift, first, first_shift, second, second_shift, final, final_shift):
    seqs, here, _ = x.shape
    width = first.shape[1]
    wide = x.astype(F32)
    centered = wide - jnp.mean(wide, axis=-1, keepdims=True)
    variance = jnp.mean(centered * centered, axis=-1, keepdims=True)
    normed = (centered * lax.rsqrt(variance + 1e-05) * gain + shift).astype(BF16)
    left = (jnp.einsum("src,ck->rsk", normed, first, preferred_element_type=F32) + first_shift).astype(BF16)
    right = (jnp.einsum("src,ck->rks", normed, second, preferred_element_type=F32) + second_shift[:, None]).astype(BF16)
    right = right.reshape(here, width, seqs // RUN, RUN).transpose(0, 2, 1, 3).reshape(here, seqs * width)
    left = lax.all_gather(left.reshape(here, seqs * width), "col", axis=0, tiled=True)
    groups = LANES // width
    left = left.reshape(groups, -1, width).transpose(1, 0, 2).reshape(-1, LANES)
    every = lax.all_gather(right, ("row", "col"), axis=0, tiled=True)
    span = every.shape[0] // lax.axis_size("col")
    mine = lax.dynamic_slice_in_dim(every, lax.axis_index("col") * span, span, 0)
    spread_left, _ = spread(left, final, seqs, width)
    return combine([spread_left], [mine], (0,), (1,), final_shift, seqs, span)


def per_device(x, gain, shift, first, first_shift, second, second_shift, final, final_shift):
    seqs, here, _ = x.shape
    width = first.shape[1]
    if (lax.axis_size("row"), lax.axis_size("col"), here % 24) != (16, 2, 0):
        return plain(x, gain, shift, first, first_shift, second, second_shift, final, final_shift)
    right, left, final = project(x, gain, shift, first, first_shift, second, second_shift, final)
    both = ("row", "col")
    far = lax.ppermute(right, both, linear(lambda r, c, i: (r ^ 1, c) if i else (r ^ 8, 1 - c)))
    near = lax.ppermute(right, both, linear(lambda r, c, i: (r ^ 8, c) if i else (r, 1 - c)))
    own, pairs = spread(left, keep(final), seqs, width)
    beside = lax.ppermute(after([left], keep(pairs))[0], "col", [(0, 1), (1, 0)])
    pair = arrange(right, near, far, pairs)
    first, second, third = [flip(pair, bits) for bits in (2, 4, 6)]
    lefts = [own, spread(beside, final, seqs, width, pairs)]
    span = 16 * here
    some, masks, total = [pair, flip(pair, 1)], (0, 1), 2 * here
    begun = combine(lefts[:1], some, masks, (2,), final_shift, seqs, span, None, 0, total)
    begun = combine(lefts[1:], some, masks, (2,), final_shift, seqs, span, begun, here // 2, total)
    pieces = after([first, second, third], keep(begun))
    begun = combine(lefts[:1], pieces, (2, 4, 6), (3,), final_shift, seqs, span, begun, 0, total)
    pieces = [flip(piece, 1) for piece in pieces] + [*pieces]
    return combine(lefts, pieces, (3, 5, 7, 2, 4, 6), (3, 6), final_shift, seqs, span, begun)


def solution(mesh):
    return jax.shard_map(
        per_device,
        mesh=mesh,
        in_specs=(P("groups", ("row", "col"), None), P(), P(), P(), P(), P(), P(), P(), P()),
        out_specs=P(("groups", "row"), "col", None),
        check_vma=False,
    )
```

```python
import functools

import jax
import jax.numpy as jnp
from jax import lax
from jax.experimental import pallas as pl
from jax.experimental.pallas import tpu as pltpu
from jax.sharding import PartitionSpec as P

F32, BF16 = jnp.float32, jnp.bfloat16
LANES = 128
RUN = 8


def project_kernel(*refs):
    sources, (r_ref, l_ref, final_ref, held), buffers, sems = refs[:8], refs[8:12], refs[12:19], refs[19]
    targets = (*buffers, final_ref)
    copies = [pltpu.make_async_copy(src, dst, sems.at[k]) for k, (src, dst) in enumerate(zip(sources, targets))]
    for copy in copies:
        copy.start()
    for copy in copies[:-1]:
        copy.wait()
    x_ref, gain_ref, shift_ref, left_ref, left_shift_ref, right_ref, right_shift_ref = buffers
    seqs, here, channels = x_ref.shape
    width = left_ref.shape[0]
    groups = LANES // width
    x = x_ref[...].astype(F32).reshape(seqs * here, channels)
    centered = x - jnp.mean(x, axis=-1, keepdims=True)
    variance = jnp.mean(centered * centered, axis=-1, keepdims=True)
    normed = (centered * lax.rsqrt(variance + 1e-05) * gain_ref[...] + shift_ref[...]).astype(BF16)
    matrices = jnp.concatenate([left_ref[...]] * groups + [right_ref[...]] * groups, axis=0)
    shifts = jnp.concatenate([left_shift_ref[...]] * groups + [right_shift_ref[...]] * groups, axis=1)
    both = lax.dot_general(normed, matrices, (((1,), (1,)), ((), ())), preferred_element_type=F32) + shifts
    held[0], held[1] = both[:, :LANES], both[:, LANES:]
    group = lax.broadcasted_iota(jnp.int32, (1, LANES), 1) // width
    per = here // groups
    for i in range(per):
        packed = held[0, pl.ds(i, seqs, stride=here), :]
        for g in range(1, groups):
            packed = jnp.where(group == g, held[0, pl.ds(g * per + i, seqs, stride=here), :], packed)
        l_ref[i * seqs : (i + 1) * seqs, :] = packed.astype(BF16)
    rows = []
    for q in range(seqs // RUN):
        tiles = []
        for t in range(RUN // groups):
            s = q * RUN + t * groups
            packed = held[1, s * here : (s + 1) * here, :]
            for g in range(1, groups):
                packed = jnp.where(group == g, held[1, (s + g) * here : (s + g + 1) * here, :], packed)
            tiles.append(packed)
        rows.append(jnp.concatenate(tiles, axis=1))
    packed = jnp.concatenate(rows, axis=0).astype(BF16)
    span = RUN * width
    a = lax.broadcasted_iota(jnp.int32, (span, span), 0)
    b = lax.broadcasted_iota(jnp.int32, (span, span), 1)
    order = jnp.where((a % width) * RUN + a // width == b, 1.0, 0.0).astype(BF16)
    ordered = jnp.dot(packed, order, preferred_element_type=F32).astype(BF16)
    for q in range(seqs // RUN):
        r_ref[:, q * span : (q + 1) * span] = ordered[q * here : (q + 1) * here, :]
    copies[-1].wait()


def spread_left(seqs, width, l_ref, pairs, t_ref):
    groups = LANES // width
    residues = l_ref.shape[0] // seqs * groups
    left = jnp.concatenate([l_ref[:, g * width : (g + 1) * width] for g in range(groups)], axis=0)
    for m in range(width // 2):
        wide_out = jnp.dot(left, pairs[m], preferred_element_type=F32)
        for i in range(residues):
            for q in range(seqs // RUN):
                s = i * seqs + q * RUN
                block = jnp.concatenate([wide_out[s : s + RUN, :LANES], wide_out[s : s + RUN, LANES:]], axis=0)
                start = q * RUN * width + m * 2 * RUN
                t_ref[i // 2, start : start + 2 * RUN, (i % 2) * LANES : (i % 2 + 1) * LANES] = block.astype(BF16)


def spread_first_kernel(seqs, width, l_ref, f_ref, t_ref, pairs, wide):
    wide[...] = f_ref[...].astype(F32)
    for d in range(width):
        pairs[d // 2, :, (d % 2) * LANES : (d % 2 + 1) * LANES] = wide[pl.ds(d, width, stride=width), :].astype(BF16)
    spread_left(seqs, width, l_ref, pairs, t_ref)


def spread_second_kernel(seqs, width, l_ref, pairs, t_ref):
    spread_left(seqs, width, l_ref, pairs, t_ref)


def arrange_kernel(own_ref, near_ref, far_ref, _, pair_ref):
    row, col = lax.axis_index("row"), lax.axis_index("col")
    inside = row // 8 == col
    here = own_ref.shape[0]
    own, near, far = own_ref[...], near_ref[...], far_ref[...]
    same, other = jnp.where(inside, own, near), jnp.where(inside, near, far)
    pair_ref[:here, :] = jnp.where(col == 0, same, other)
    pair_ref[here:, :] = jnp.where(col == 0, other, same)


def order_kernel(*refs):
    pass


def join_kernel(count, *refs):
    rows = refs[0].shape[0]
    for n in range(count):
        refs[-1][n * rows : (n + 1) * rows, :] = refs[n][...]


def combine_kernel(seqs, rows, n_pieces, masks, counts, offset, last, begun, *refs):
    refs = refs[begun:]
    lefts, pieces = refs[1 : 1 + len(counts)], refs[1 + len(counts) : 1 + len(counts) + n_pieces]
    shift_ref, stage, right = refs[0], refs[-3], refs[-2]
    pairs = lefts[0].shape[0]
    spots = stage.shape[2] // rows
    spot = lax.rem(lax.axis_index("row"), spots) if spots > 1 else 0
    places = [pl.multiple_of(jnp.bitwise_xor(spot, mask) * rows, rows) if spots > 1 else 0 for mask in masks]
    if n_pieces == 1:
        right = pieces[0]
    else:
        start = 0
        for piece in pieces:
            right[start : start + piece.shape[0], :] = piece[...]
            start += piece.shape[0]
    shift = jnp.concatenate([shift_ref[...]] * 2, axis=1)
    unroll = next(u for u in (12, 6, 4, 3, 2, 1) if pairs % u == 0)

    for h, (left, count) in enumerate(zip(lefts, counts)):
        first = 2 * pairs * (jnp.bitwise_xor(lax.axis_index("col"), h) if len(lefts) > 1 else 0)

        def step(n, carry, left=left, first=first, count=count, h=h):
            for u in range(unroll):
                p = n * unroll + u
                update = jnp.dot(right[: count * rows, :], left[p], preferred_element_type=F32) * (1.0 / seqs) + shift
                for k, place in enumerate(places[:count]):
                    block = update[k * rows : (k + 1) * rows].astype(BF16)
                    stage[offset + h * pairs + p, 0, pl.ds(place, rows)] = block[:, :LANES]
                    stage[offset + h * pairs + p, 1, pl.ds(place, rows)] = block[:, LANES:]
                if last:
                    out_ref, sem = refs[-4], refs[-1]
                    pltpu.make_async_copy(stage.at[h * pairs + p], out_ref.at[pl.ds(first + 2 * p, 2)], sem).start()
            return carry

        lax.fori_loop(0, pairs // unroll, step, 0)
    if last:
        out_ref, sem = refs[-4], refs[-1]
        pltpu.make_async_copy(out_ref, out_ref, sem).wait()


VMEM = pl.BlockSpec(memory_space=pltpu.VMEM)
HBM = pl.BlockSpec(memory_space=pltpu.HBM)


def params():
    return pltpu.CompilerParams(vmem_limit_bytes=12 << 20)


def keep(value):
    return pltpu.with_memory_space_constraint(value, pltpu.VMEM)


def project(x, gain, shift, first, first_shift, second, second_shift, final):
    seqs, here, channels = x.shape
    width = first.shape[1]
    args = (x, gain[None], shift[None], first.T, first_shift[None], second.T, second_shift[None], final)
    args = [pltpu.with_memory_space_constraint(a, pltpu.HBM) for a in args]
    return pl.pallas_call(
        project_kernel,
        out_shape=(
            jax.ShapeDtypeStruct((here, seqs * width), BF16),
            jax.ShapeDtypeStruct((here * width // LANES * seqs, LANES), BF16),
            pltpu.VMEM(final.shape, BF16),
        ),
        in_specs=[HBM] * len(args),
        out_specs=(VMEM, VMEM, VMEM),
        scratch_shapes=[pltpu.VMEM((2, seqs * here, LANES), F32)]
        + [pltpu.VMEM(a.shape, a.dtype) for a in args[:-1]]
        + [pltpu.SemaphoreType.DMA((len(args),))],
        compiler_params=params(),
        cost_estimate=pl.CostEstimate(flops=2 * x.size * 256, bytes_accessed=2 * x.size, transcendentals=0),
        name="project",
    )(*args)


def spread(left, final, seqs, width, pairs=None):
    residues = left.shape[0] // seqs * (LANES // width)
    wide = pltpu.VMEM((residues // 2, seqs * width, 2 * LANES), BF16)
    cost = pl.CostEstimate(
        flops=2 * residues * seqs * 256 * width * LANES, bytes_accessed=left.size * 2, transcendentals=0
    )
    if pairs is None:
        return pl.pallas_call(
            functools.partial(spread_first_kernel, seqs, width),
            out_shape=(wide, pltpu.VMEM((width // 2, width, 2 * LANES), BF16)),
            in_specs=[VMEM] * 2,
            out_specs=(VMEM, VMEM),
            scratch_shapes=[pltpu.VMEM(final.shape, F32)],
            compiler_params=params(),
            cost_estimate=cost,
            name="spread_first",
        )(left, final)
    return pl.pallas_call(
        functools.partial(spread_second_kernel, seqs, width),
        out_shape=wide,
        in_specs=[VMEM] * 2,
        out_specs=VMEM,
        compiler_params=params(),
        cost_estimate=cost,
        name="spread_second",
    )(left, keep(pairs))


def arrange(own, near, far, after):
    return pl.pallas_call(
        arrange_kernel,
        out_shape=jax.ShapeDtypeStruct((2 * own.shape[0], own.shape[1]), BF16),
        in_specs=[VMEM] * 4,
        out_specs=VMEM,
        compiler_params=params(),
        name="arrange",
    )(own, near, far, keep(after))


def after(values, *earlier):
    n = len(values)
    return pl.pallas_call(
        order_kernel,
        out_shape=[jax.ShapeDtypeStruct(v.shape, v.dtype) for v in values],
        in_specs=[pl.BlockSpec(memory_space=pl.ANY)] * (n + len(earlier)),
        out_specs=[pl.BlockSpec(memory_space=pl.ANY)] * n,
        input_output_aliases={k: k for k in range(n)},
        compiler_params=params(),
        name="after",
    )(*values, *earlier)


def join(values, *earlier):
    rows, depth = values[0].shape
    return pl.pallas_call(
        functools.partial(join_kernel, len(values)),
        out_shape=jax.ShapeDtypeStruct((len(values) * rows, depth), BF16),
        in_specs=[VMEM] * (len(values) + len(earlier)),
        out_specs=VMEM,
        compiler_params=params(),
        name="join",
    )(*values, *[keep(e) for e in earlier])


def combine(lefts, pieces, masks, counts, final_shift, seqs, span, begun=None, offset=0, total=None):
    last = total is None
    pairs, depth, _ = lefts[0].shape
    rows = sum(piece.shape[0] for piece in pieces) // len(masks)
    total = total or 2 * pairs * len(lefts)
    stage = pltpu.VMEM((total // 2, 2, span, LANES), BF16)
    args = [] if begun is None else [keep(begun)]
    args += [final_shift[None], *[keep(left) for left in lefts], *pieces]
    outs = ([jax.ShapeDtypeStruct((total, span, LANES), BF16)] if last else []) + [stage]
    return pl.pallas_call(
        functools.partial(combine_kernel, seqs, rows, len(pieces), masks, counts, offset, last, 0 if begun is None else 1),
        out_shape=outs,
        in_specs=[VMEM] * len(args),
        out_specs=[HBM, VMEM] if last else [VMEM],
        input_output_aliases={} if begun is None else {0: len(outs) - 1},
        scratch_shapes=[pltpu.VMEM((rows * len(masks), depth), BF16), pltpu.SemaphoreType.DMA],
        compiler_params=params(),
        cost_estimate=pl.CostEstimate(
            flops=4 * pairs * sum(counts) * rows * LANES * depth, bytes_accessed=0, transcendentals=0
        ),
        name="combine_last" if last else "combine_some",
    )(*args)[0]


def linear(target):
    moves = []
    for r in range(16):
        for c in range(2):
            t = target(r, c, r // 8 == c)
            if t is not None:
                moves.append((r * 2 + c, t[0] * 2 + t[1]))
    return moves


def flip(value, bits):
    return lax.ppermute(value, "row", [(r, r ^ bits) for r in range(16)])


def plain(x, gain, shift, first, first_shift, second, second_shift, final, final_shift):
    seqs, here, _ = x.shape
    width = first.shape[1]
    wide = x.astype(F32)
    centered = wide - jnp.mean(wide, axis=-1, keepdims=True)
    variance = jnp.mean(centered * centered, axis=-1, keepdims=True)
    normed = (centered * lax.rsqrt(variance + 1e-05) * gain + shift).astype(BF16)
    left = (jnp.einsum("src,ck->rsk", normed, first, preferred_element_type=F32) + first_shift).astype(BF16)
    right = (jnp.einsum("src,ck->rks", normed, second, preferred_element_type=F32) + second_shift[:, None]).astype(BF16)
    right = right.reshape(here, width, seqs // RUN, RUN).transpose(0, 2, 1, 3).reshape(here, seqs * width)
    left = lax.all_gather(left.reshape(here, seqs * width), "col", axis=0, tiled=True)
    groups = LANES // width
    left = left.reshape(groups, -1, width).transpose(1, 0, 2).reshape(-1, LANES)
    every = lax.all_gather(right, ("row", "col"), axis=0, tiled=True)
    span = every.shape[0] // lax.axis_size("col")
    mine = lax.dynamic_slice_in_dim(every, lax.axis_index("col") * span, span, 0)
    spread_left, _ = spread(left, final, seqs, width)
    return combine([spread_left], [mine], (0,), (1,), final_shift, seqs, span)


def per_device(x, gain, shift, first, first_shift, second, second_shift, final, final_shift):
    seqs, here, _ = x.shape
    width = first.shape[1]
    if (lax.axis_size("row"), lax.axis_size("col"), here % 24) != (16, 2, 0):
        return plain(x, gain, shift, first, first_shift, second, second_shift, final, final_shift)
    right, left, final = project(x, gain, shift, first, first_shift, second, second_shift, final)
    both = ("row", "col")
    far = lax.ppermute(right, both, linear(lambda r, c, i: (r ^ 1, c) if i else (r ^ 8, 1 - c)))
    near = lax.ppermute(right, both, linear(lambda r, c, i: (r ^ 8, c) if i else (r, 1 - c)))
    own, pairs = spread(left, keep(final), seqs, width)
    beside = lax.ppermute(after([left], keep(pairs))[0], "col", [(0, 1), (1, 0)])
    pair = arrange(right, near, far, pairs)
    first, second, third = [flip(pair, bits) for bits in (2, 4, 6)]
    lefts = [own, spread(beside, final, seqs, width, pairs)]
    span = 16 * here
    some, masks, total = [pair, flip(pair, 1)], (0, 1), 2 * here
    begun = combine(lefts[:1], some, masks, (2,), final_shift, seqs, span, None, 0, total)
    begun = combine(lefts[1:], some, masks, (2,), final_shift, seqs, span, begun, here // 2, total)
    three = join([first, second, third], begun)
    begun = combine(lefts[:1], [three], (2, 4, 6), (3,), final_shift, seqs, span, begun, 0, total)
    return combine(lefts, [flip(three, 1), three], (3, 5, 7, 2, 4, 6), (3, 6), final_shift, seqs, span, begun)


def solution(mesh):
    return jax.shard_map(
        per_device,
        mesh=mesh,
        in_specs=(P("groups", ("row", "col"), None), P(), P(), P(), P(), P(), P(), P(), P()),
        out_specs=P(("groups", "row"), "col", None),
        check_vma=False,
    )
```

```python
import functools

import jax
import jax.numpy as jnp
from jax import lax
from jax.experimental import pallas as pl
from jax.experimental.pallas import tpu as pltpu
from jax.sharding import PartitionSpec as P

F32, BF16 = jnp.float32, jnp.bfloat16
LANES = 128
RUN = 8


def project_kernel(*refs):
    sources, (r_ref, l_ref, final_ref, held), buffers, sems = refs[:8], refs[8:12], refs[12:19], refs[19]
    targets = (*buffers, final_ref)
    copies = [pltpu.make_async_copy(src, dst, sems.at[k]) for k, (src, dst) in enumerate(zip(sources, targets))]
    for copy in copies:
        copy.start()
    for copy in copies[:-1]:
        copy.wait()
    x_ref, gain_ref, shift_ref, left_ref, left_shift_ref, right_ref, right_shift_ref = buffers
    seqs, here, channels = x_ref.shape
    width = left_ref.shape[0]
    groups = LANES // width
    x = x_ref[...].astype(F32).reshape(seqs * here, channels)
    centered = x - jnp.mean(x, axis=-1, keepdims=True)
    variance = jnp.mean(centered * centered, axis=-1, keepdims=True)
    normed = (centered * lax.rsqrt(variance + 1e-05) * gain_ref[...] + shift_ref[...]).astype(BF16)
    matrices = jnp.concatenate([left_ref[...]] * groups + [right_ref[...]] * groups, axis=0)
    shifts = jnp.concatenate([left_shift_ref[...]] * groups + [right_shift_ref[...]] * groups, axis=1)
    both = lax.dot_general(normed, matrices, (((1,), (1,)), ((), ())), preferred_element_type=F32) + shifts
    held[0], held[1] = both[:, :LANES], both[:, LANES:]
    group = lax.broadcasted_iota(jnp.int32, (1, LANES), 1) // width
    per = here // groups
    for i in range(per):
        packed = held[0, pl.ds(i, seqs, stride=here), :]
        for g in range(1, groups):
            packed = jnp.where(group == g, held[0, pl.ds(g * per + i, seqs, stride=here), :], packed)
        l_ref[i * seqs : (i + 1) * seqs, :] = packed.astype(BF16)
    rows = []
    for q in range(seqs // RUN):
        tiles = []
        for t in range(RUN // groups):
            s = q * RUN + t * groups
            packed = held[1, s * here : (s + 1) * here, :]
            for g in range(1, groups):
                packed = jnp.where(group == g, held[1, (s + g) * here : (s + g + 1) * here, :], packed)
            tiles.append(packed)
        rows.append(jnp.concatenate(tiles, axis=1))
    packed = jnp.concatenate(rows, axis=0).astype(BF16)
    span = RUN * width
    a = lax.broadcasted_iota(jnp.int32, (span, span), 0)
    b = lax.broadcasted_iota(jnp.int32, (span, span), 1)
    order = jnp.where((a % width) * RUN + a // width == b, 1.0, 0.0).astype(BF16)
    ordered = jnp.dot(packed, order, preferred_element_type=F32).astype(BF16)
    for q in range(seqs // RUN):
        r_ref[:, q * span : (q + 1) * span] = ordered[q * here : (q + 1) * here, :]
    copies[-1].wait()


def spread_left(seqs, width, l_ref, pairs, t_ref):
    groups = LANES // width
    residues = l_ref.shape[0] // seqs * groups
    left = jnp.concatenate([l_ref[:, g * width : (g + 1) * width] for g in range(groups)], axis=0)
    for m in range(width // 2):
        wide_out = jnp.dot(left, pairs[m], preferred_element_type=F32)
        for i in range(residues):
            for q in range(seqs // RUN):
                s = i * seqs + q * RUN
                block = jnp.concatenate([wide_out[s : s + RUN, :LANES], wide_out[s : s + RUN, LANES:]], axis=0)
                start = q * RUN * width + m * 2 * RUN
                t_ref[i // 2, start : start + 2 * RUN, (i % 2) * LANES : (i % 2 + 1) * LANES] = block.astype(BF16)


def spread_first_kernel(seqs, width, l_ref, f_ref, t_ref, pairs, wide):
    wide[...] = f_ref[...].astype(F32)
    for d in range(width):
        pairs[d // 2, :, (d % 2) * LANES : (d % 2 + 1) * LANES] = wide[pl.ds(d, width, stride=width), :].astype(BF16)
    spread_left(seqs, width, l_ref, pairs, t_ref)


def spread_second_kernel(seqs, width, l_ref, pairs, t_ref):
    spread_left(seqs, width, l_ref, pairs, t_ref)


def arrange_kernel(own_ref, near_ref, far_ref, _, pair_ref):
    row, col = lax.axis_index("row"), lax.axis_index("col")
    inside = row // 8 == col
    here = own_ref.shape[0]
    own, near, far = own_ref[...], near_ref[...], far_ref[...]
    same, other = jnp.where(inside, own, near), jnp.where(inside, near, far)
    pair_ref[:here, :] = jnp.where(col == 0, same, other)
    pair_ref[here:, :] = jnp.where(col == 0, other, same)


def order_kernel(*refs):
    pass


def join_kernel(count, *refs):
    rows = refs[0].shape[0]
    for n in range(count):
        refs[-1][n * rows : (n + 1) * rows, :] = refs[n][...]


def combine_kernel(seqs, rows, n_pieces, masks, counts, offset, last, begun, *refs):
    refs = refs[begun:]
    lefts, pieces = refs[1 : 1 + len(counts)], refs[1 + len(counts) : 1 + len(counts) + n_pieces]
    shift_ref, stage, right = refs[0], refs[-3], refs[-2]
    pairs = lefts[0].shape[0]
    spots = stage.shape[2] // rows
    spot = lax.rem(lax.axis_index("row"), spots) if spots > 1 else 0
    places = [pl.multiple_of(jnp.bitwise_xor(spot, mask) * rows, rows) if spots > 1 else 0 for mask in masks]
    if n_pieces == 1:
        right = pieces[0]
    else:
        start = 0
        for piece in pieces:
            right[start : start + piece.shape[0], :] = piece[...]
            start += piece.shape[0]
    shift = jnp.concatenate([shift_ref[...]] * 2, axis=1)
    unroll = next(u for u in (12, 6, 4, 3, 2, 1) if pairs % u == 0)

    for h, (left, count) in enumerate(zip(lefts, counts)):
        first = 2 * pairs * (jnp.bitwise_xor(lax.axis_index("col"), h) if len(lefts) > 1 else 0)

        def step(n, carry, left=left, first=first, count=count, h=h):
            for u in range(unroll):
                p = n * unroll + u
                update = jnp.dot(right[: count * rows, :], left[p], preferred_element_type=F32) * (1.0 / seqs) + shift
                for k, place in enumerate(places[:count]):
                    block = update[k * rows : (k + 1) * rows].astype(BF16)
                    stage[offset + h * pairs + p, 0, pl.ds(place, rows)] = block[:, :LANES]
                    stage[offset + h * pairs + p, 1, pl.ds(place, rows)] = block[:, LANES:]
                if last:
                    out_ref, sem = refs[-4], refs[-1]
                    pltpu.make_async_copy(stage.at[h * pairs + p], out_ref.at[pl.ds(first + 2 * p, 2)], sem).start()
            return carry

        lax.fori_loop(0, pairs // unroll, step, 0)
    if last:
        out_ref, sem = refs[-4], refs[-1]
        pltpu.make_async_copy(out_ref, out_ref, sem).wait()


VMEM = pl.BlockSpec(memory_space=pltpu.VMEM)
HBM = pl.BlockSpec(memory_space=pltpu.HBM)


def params():
    return pltpu.CompilerParams(vmem_limit_bytes=12 << 20)


def keep(value):
    return pltpu.with_memory_space_constraint(value, pltpu.VMEM)


def project(x, gain, shift, first, first_shift, second, second_shift, final):
    seqs, here, channels = x.shape
    width = first.shape[1]
    args = (x, gain[None], shift[None], first.T, first_shift[None], second.T, second_shift[None], final)
    args = [pltpu.with_memory_space_constraint(a, pltpu.HBM) for a in args]
    return pl.pallas_call(
        project_kernel,
        out_shape=(
            jax.ShapeDtypeStruct((here, seqs * width), BF16),
            jax.ShapeDtypeStruct((here * width // LANES * seqs, LANES), BF16),
            pltpu.VMEM(final.shape, BF16),
        ),
        in_specs=[HBM] * len(args),
        out_specs=(VMEM, VMEM, VMEM),
        scratch_shapes=[pltpu.VMEM((2, seqs * here, LANES), F32)]
        + [pltpu.VMEM(a.shape, a.dtype) for a in args[:-1]]
        + [pltpu.SemaphoreType.DMA((len(args),))],
        compiler_params=params(),
        cost_estimate=pl.CostEstimate(flops=2 * x.size * 256, bytes_accessed=2 * x.size, transcendentals=0),
        name="project",
    )(*args)


def spread(left, final, seqs, width, pairs=None):
    residues = left.shape[0] // seqs * (LANES // width)
    wide = pltpu.VMEM((residues // 2, seqs * width, 2 * LANES), BF16)
    cost = pl.CostEstimate(
        flops=2 * residues * seqs * 256 * width * LANES, bytes_accessed=left.size * 2, transcendentals=0
    )
    if pairs is None:
        return pl.pallas_call(
            functools.partial(spread_first_kernel, seqs, width),
            out_shape=(wide, pltpu.VMEM((width // 2, width, 2 * LANES), BF16)),
            in_specs=[VMEM] * 2,
            out_specs=(VMEM, VMEM),
            scratch_shapes=[pltpu.VMEM(final.shape, F32)],
            compiler_params=params(),
            cost_estimate=cost,
            name="spread_first",
        )(left, final)
    return pl.pallas_call(
        functools.partial(spread_second_kernel, seqs, width),
        out_shape=wide,
        in_specs=[VMEM] * 2,
        out_specs=VMEM,
        compiler_params=params(),
        cost_estimate=cost,
        name="spread_second",
    )(left, keep(pairs))


def arrange(own, near, far, after):
    return pl.pallas_call(
        arrange_kernel,
        out_shape=jax.ShapeDtypeStruct((2 * own.shape[0], own.shape[1]), BF16),
        in_specs=[VMEM] * 4,
        out_specs=VMEM,
        compiler_params=params(),
        name="arrange",
    )(own, near, far, keep(after))


def after(values, *earlier):
    n = len(values)
    return pl.pallas_call(
        order_kernel,
        out_shape=[jax.ShapeDtypeStruct(v.shape, v.dtype) for v in values],
        in_specs=[pl.BlockSpec(memory_space=pl.ANY)] * (n + len(earlier)),
        out_specs=[pl.BlockSpec(memory_space=pl.ANY)] * n,
        input_output_aliases={k: k for k in range(n)},
        compiler_params=params(),
        name="after",
    )(*values, *earlier)


def join(values, *earlier):
    rows, depth = values[0].shape
    return pl.pallas_call(
        functools.partial(join_kernel, len(values)),
        out_shape=jax.ShapeDtypeStruct((len(values) * rows, depth), BF16),
        in_specs=[VMEM] * (len(values) + len(earlier)),
        out_specs=VMEM,
        compiler_params=params(),
        name="join",
    )(*values, *[keep(e) for e in earlier])


def combine(lefts, pieces, masks, counts, final_shift, seqs, span, begun=None, offset=0, total=None):
    last = total is None
    pairs, depth, _ = lefts[0].shape
    rows = sum(piece.shape[0] for piece in pieces) // len(masks)
    total = total or 2 * pairs * len(lefts)
    stage = pltpu.VMEM((total // 2, 2, span, LANES), BF16)
    args = [] if begun is None else [keep(begun)]
    args += [final_shift[None], *[keep(left) for left in lefts], *pieces]
    outs = ([jax.ShapeDtypeStruct((total, span, LANES), BF16)] if last else []) + [stage]
    return pl.pallas_call(
        functools.partial(combine_kernel, seqs, rows, len(pieces), masks, counts, offset, last, 0 if begun is None else 1),
        out_shape=outs,
        in_specs=[VMEM] * len(args),
        out_specs=[HBM, VMEM] if last else [VMEM],
        input_output_aliases={} if begun is None else {0: len(outs) - 1},
        scratch_shapes=[pltpu.VMEM((rows * len(masks), depth), BF16), pltpu.SemaphoreType.DMA],
        compiler_params=params(),
        cost_estimate=pl.CostEstimate(
            flops=4 * pairs * sum(counts) * rows * LANES * depth, bytes_accessed=0, transcendentals=0
        ),
        name="combine_last" if last else "combine_some",
    )(*args)[0]


def linear(target):
    moves = []
    for r in range(16):
        for c in range(2):
            t = target(r, c, r // 8 == c)
            if t is not None:
                moves.append((r * 2 + c, t[0] * 2 + t[1]))
    return moves


def flip(value, bits):
    return lax.ppermute(value, "row", [(r, r ^ bits) for r in range(16)])


def plain(x, gain, shift, first, first_shift, second, second_shift, final, final_shift):
    seqs, here, _ = x.shape
    width = first.shape[1]
    wide = x.astype(F32)
    centered = wide - jnp.mean(wide, axis=-1, keepdims=True)
    variance = jnp.mean(centered * centered, axis=-1, keepdims=True)
    normed = (centered * lax.rsqrt(variance + 1e-05) * gain + shift).astype(BF16)
    left = (jnp.einsum("src,ck->rsk", normed, first, preferred_element_type=F32) + first_shift).astype(BF16)
    right = (jnp.einsum("src,ck->rks", normed, second, preferred_element_type=F32) + second_shift[:, None]).astype(BF16)
    right = right.reshape(here, width, seqs // RUN, RUN).transpose(0, 2, 1, 3).reshape(here, seqs * width)
    left = lax.all_gather(left.reshape(here, seqs * width), "col", axis=0, tiled=True)
    groups = LANES // width
    left = left.reshape(groups, -1, width).transpose(1, 0, 2).reshape(-1, LANES)
    every = lax.all_gather(right, ("row", "col"), axis=0, tiled=True)
    span = every.shape[0] // lax.axis_size("col")
    mine = lax.dynamic_slice_in_dim(every, lax.axis_index("col") * span, span, 0)
    spread_left, _ = spread(left, final, seqs, width)
    return combine([spread_left], [mine], (0,), (1,), final_shift, seqs, span)


def per_device(x, gain, shift, first, first_shift, second, second_shift, final, final_shift):
    seqs, here, _ = x.shape
    width = first.shape[1]
    if (lax.axis_size("row"), lax.axis_size("col"), here % 24) != (16, 2, 0):
        return plain(x, gain, shift, first, first_shift, second, second_shift, final, final_shift)
    right, left, final = project(x, gain, shift, first, first_shift, second, second_shift, final)
    both = ("row", "col")
    far = lax.ppermute(right, both, linear(lambda r, c, i: (r ^ 1, c) if i else (r ^ 8, 1 - c)))
    near = lax.ppermute(right, both, linear(lambda r, c, i: (r ^ 8, c) if i else (r, 1 - c)))
    own, pairs = spread(left, keep(final), seqs, width)
    beside = lax.ppermute(after([left], keep(pairs))[0], "col", [(0, 1), (1, 0)])
    pair = arrange(right, near, far, pairs)
    first, second, third = [flip(pair, bits) for bits in (2, 4, 6)]
    lefts = [own, spread(beside, final, seqs, width, pairs)]
    span = 16 * here
    some, masks, total = [pair, flip(pair, 1)], (0, 1), 2 * here
    begun = combine(lefts, some, masks, (2, 2), final_shift, seqs, span, None, 0, total)
    three = join([first, second, third], begun)
    begun = combine(lefts[:1], [three], (2, 4, 6), (3,), final_shift, seqs, span, begun, 0, total)
    return combine(lefts, [flip(three, 1), three], (3, 5, 7, 2, 4, 6), (3, 6), final_shift, seqs, span, begun)


def solution(mesh):
    return jax.shard_map(
        per_device,
        mesh=mesh,
        in_specs=(P("groups", ("row", "col"), None), P(), P(), P(), P(), P(), P(), P(), P()),
        out_specs=P(("groups", "row"), "col", None),
        check_vma=False,
    )
```

```python
import functools

import jax
import jax.numpy as jnp
from jax import lax
from jax.experimental import pallas as pl
from jax.experimental.pallas import tpu as pltpu
from jax.sharding import PartitionSpec as P

F32, BF16 = jnp.float32, jnp.bfloat16
LANES = 128
RUN = 8


def project_kernel(*refs):
    sources, (r_ref, l_ref, final_ref, held), buffers, sems = refs[:8], refs[8:12], refs[12:19], refs[19]
    targets = (*buffers, final_ref)
    copies = [pltpu.make_async_copy(src, dst, sems.at[k]) for k, (src, dst) in enumerate(zip(sources, targets))]
    for copy in copies:
        copy.start()
    for copy in copies[:-1]:
        copy.wait()
    x_ref, gain_ref, shift_ref, left_ref, left_shift_ref, right_ref, right_shift_ref = buffers
    seqs, here, channels = x_ref.shape
    width = left_ref.shape[0]
    groups = LANES // width
    x = x_ref[...].astype(F32).reshape(seqs * here, channels)
    centered = x - jnp.mean(x, axis=-1, keepdims=True)
    variance = jnp.mean(centered * centered, axis=-1, keepdims=True)
    normed = (centered * lax.rsqrt(variance + 1e-05) * gain_ref[...] + shift_ref[...]).astype(BF16)
    matrices = jnp.concatenate([left_ref[...]] * groups + [right_ref[...]] * groups, axis=0)
    shifts = jnp.concatenate([left_shift_ref[...]] * groups + [right_shift_ref[...]] * groups, axis=1)
    both = lax.dot_general(normed, matrices, (((1,), (1,)), ((), ())), preferred_element_type=F32) + shifts
    held[0], held[1] = both[:, :LANES], both[:, LANES:]
    group = lax.broadcasted_iota(jnp.int32, (1, LANES), 1) // width
    per = here // groups
    for i in range(per):
        packed = held[0, pl.ds(i, seqs, stride=here), :]
        for g in range(1, groups):
            packed = jnp.where(group == g, held[0, pl.ds(g * per + i, seqs, stride=here), :], packed)
        l_ref[i * seqs : (i + 1) * seqs, :] = packed.astype(BF16)
    rows = []
    for q in range(seqs // RUN):
        tiles = []
        for t in range(RUN // groups):
            s = q * RUN + t * groups
            packed = held[1, s * here : (s + 1) * here, :]
            for g in range(1, groups):
                packed = jnp.where(group == g, held[1, (s + g) * here : (s + g + 1) * here, :], packed)
            tiles.append(packed)
        rows.append(jnp.concatenate(tiles, axis=1))
    packed = jnp.concatenate(rows, axis=0).astype(BF16)
    span = RUN * width
    a = lax.broadcasted_iota(jnp.int32, (span, span), 0)
    b = lax.broadcasted_iota(jnp.int32, (span, span), 1)
    order = jnp.where((a % width) * RUN + a // width == b, 1.0, 0.0).astype(BF16)
    ordered = jnp.dot(packed, order, preferred_element_type=F32).astype(BF16)
    for q in range(seqs // RUN):
        r_ref[:, q * span : (q + 1) * span] = ordered[q * here : (q + 1) * here, :]
    copies[-1].wait()


def spread_left(seqs, width, l_ref, pairs, t_ref):
    groups = LANES // width
    residues = l_ref.shape[0] // seqs * groups
    left = jnp.concatenate([l_ref[:, g * width : (g + 1) * width] for g in range(groups)], axis=0)
    for m in range(width // 2):
        wide_out = jnp.dot(left, pairs[m], preferred_element_type=F32)
        for i in range(residues):
            for q in range(seqs // RUN):
                s = i * seqs + q * RUN
                block = jnp.concatenate([wide_out[s : s + RUN, :LANES], wide_out[s : s + RUN, LANES:]], axis=0)
                start = q * RUN * width + m * 2 * RUN
                t_ref[i // 2, start : start + 2 * RUN, (i % 2) * LANES : (i % 2 + 1) * LANES] = block.astype(BF16)


def spread_first_kernel(seqs, width, l_ref, f_ref, t_ref, pairs, wide):
    wide[...] = f_ref[...].astype(F32)
    for d in range(width):
        pairs[d // 2, :, (d % 2) * LANES : (d % 2 + 1) * LANES] = wide[pl.ds(d, width, stride=width), :].astype(BF16)
    spread_left(seqs, width, l_ref, pairs, t_ref)


def spread_second_kernel(seqs, width, l_ref, pairs, t_ref):
    spread_left(seqs, width, l_ref, pairs, t_ref)


def arrange_kernel(own_ref, near_ref, far_ref, _, pair_ref):
    row, col = lax.axis_index("row"), lax.axis_index("col")
    inside = row // 8 == col
    here = own_ref.shape[0]
    own, near, far = own_ref[...], near_ref[...], far_ref[...]
    same, other = jnp.where(inside, own, near), jnp.where(inside, near, far)
    pair_ref[:here, :] = jnp.where(col == 0, same, other)
    pair_ref[here:, :] = jnp.where(col == 0, other, same)


def order_kernel(*refs):
    pass


def join_kernel(count, *refs):
    rows = refs[0].shape[0]
    for n in range(count):
        refs[-1][n * rows : (n + 1) * rows, :] = refs[n][...]


def combine_kernel(seqs, rows, n_pieces, masks, counts, offset, last, begun, *refs):
    refs = refs[begun:]
    lefts, pieces = refs[1 : 1 + len(counts)], refs[1 + len(counts) : 1 + len(counts) + n_pieces]
    shift_ref, stage, right = refs[0], refs[-3], refs[-2]
    pairs = lefts[0].shape[0]
    spots = stage.shape[2] // rows
    spot = lax.rem(lax.axis_index("row"), spots) if spots > 1 else 0
    places = [pl.multiple_of(jnp.bitwise_xor(spot, mask) * rows, rows) if spots > 1 else 0 for mask in masks]
    if n_pieces == 1:
        right = pieces[0]
    else:
        start = 0
        for piece in pieces:
            right[start : start + piece.shape[0], :] = piece[...]
            start += piece.shape[0]
    shift = jnp.concatenate([shift_ref[...]] * 2, axis=1)
    unroll = next(u for u in (12, 6, 4, 3, 2, 1) if pairs % u == 0)

    for h, (left, count) in enumerate(zip(lefts, counts)):
        first = 2 * pairs * (jnp.bitwise_xor(lax.axis_index("col"), h) if len(lefts) > 1 else 0)

        source = pieces[0] if count * rows == pieces[0].shape[0] else right

        def step(n, carry, left=left, first=first, count=count, h=h, source=source):
            for u in range(unroll):
                p = n * unroll + u
                update = jnp.dot(source[: count * rows, :], left[p], preferred_element_type=F32) * (1.0 / seqs) + shift
                for k, place in enumerate(places[:count]):
                    block = update[k * rows : (k + 1) * rows].astype(BF16)
                    stage[offset + h * pairs + p, 0, pl.ds(place, rows)] = block[:, :LANES]
                    stage[offset + h * pairs + p, 1, pl.ds(place, rows)] = block[:, LANES:]
                if last:
                    out_ref, sem = refs[-4], refs[-1]
                    pltpu.make_async_copy(stage.at[h * pairs + p], out_ref.at[pl.ds(first + 2 * p, 2)], sem).start()
            return carry

        lax.fori_loop(0, pairs // unroll, step, 0)
    if last:
        out_ref, sem = refs[-4], refs[-1]
        pltpu.make_async_copy(out_ref, out_ref, sem).wait()


VMEM = pl.BlockSpec(memory_space=pltpu.VMEM)
HBM = pl.BlockSpec(memory_space=pltpu.HBM)


def params():
    return pltpu.CompilerParams(vmem_limit_bytes=12 << 20)


def keep(value):
    return pltpu.with_memory_space_constraint(value, pltpu.VMEM)


def project(x, gain, shift, first, first_shift, second, second_shift, final):
    seqs, here, channels = x.shape
    width = first.shape[1]
    args = (x, gain[None], shift[None], first.T, first_shift[None], second.T, second_shift[None], final)
    args = [pltpu.with_memory_space_constraint(a, pltpu.HBM) for a in args]
    return pl.pallas_call(
        project_kernel,
        out_shape=(
            jax.ShapeDtypeStruct((here, seqs * width), BF16),
            jax.ShapeDtypeStruct((here * width // LANES * seqs, LANES), BF16),
            pltpu.VMEM(final.shape, BF16),
        ),
        in_specs=[HBM] * len(args),
        out_specs=(VMEM, VMEM, VMEM),
        scratch_shapes=[pltpu.VMEM((2, seqs * here, LANES), F32)]
        + [pltpu.VMEM(a.shape, a.dtype) for a in args[:-1]]
        + [pltpu.SemaphoreType.DMA((len(args),))],
        compiler_params=params(),
        cost_estimate=pl.CostEstimate(flops=2 * x.size * 256, bytes_accessed=2 * x.size, transcendentals=0),
        name="project",
    )(*args)


def spread(left, final, seqs, width, pairs=None):
    residues = left.shape[0] // seqs * (LANES // width)
    wide = pltpu.VMEM((residues // 2, seqs * width, 2 * LANES), BF16)
    cost = pl.CostEstimate(
        flops=2 * residues * seqs * 256 * width * LANES, bytes_accessed=left.size * 2, transcendentals=0
    )
    if pairs is None:
        return pl.pallas_call(
            functools.partial(spread_first_kernel, seqs, width),
            out_shape=(wide, pltpu.VMEM((width // 2, width, 2 * LANES), BF16)),
            in_specs=[VMEM] * 2,
            out_specs=(VMEM, VMEM),
            scratch_shapes=[pltpu.VMEM(final.shape, F32)],
            compiler_params=params(),
            cost_estimate=cost,
            name="spread_first",
        )(left, final)
    return pl.pallas_call(
        functools.partial(spread_second_kernel, seqs, width),
        out_shape=wide,
        in_specs=[VMEM] * 2,
        out_specs=VMEM,
        compiler_params=params(),
        cost_estimate=cost,
        name="spread_second",
    )(left, keep(pairs))


def arrange(own, near, far, after):
    return pl.pallas_call(
        arrange_kernel,
        out_shape=jax.ShapeDtypeStruct((2 * own.shape[0], own.shape[1]), BF16),
        in_specs=[VMEM] * 4,
        out_specs=VMEM,
        compiler_params=params(),
        name="arrange",
    )(own, near, far, keep(after))


def after(values, *earlier):
    n = len(values)
    return pl.pallas_call(
        order_kernel,
        out_shape=[jax.ShapeDtypeStruct(v.shape, v.dtype) for v in values],
        in_specs=[pl.BlockSpec(memory_space=pl.ANY)] * (n + len(earlier)),
        out_specs=[pl.BlockSpec(memory_space=pl.ANY)] * n,
        input_output_aliases={k: k for k in range(n)},
        compiler_params=params(),
        name="after",
    )(*values, *earlier)


def join(values, *earlier):
    rows, depth = values[0].shape
    return pl.pallas_call(
        functools.partial(join_kernel, len(values)),
        out_shape=jax.ShapeDtypeStruct((len(values) * rows, depth), BF16),
        in_specs=[VMEM] * (len(values) + len(earlier)),
        out_specs=VMEM,
        compiler_params=params(),
        name="join",
    )(*values, *[keep(e) for e in earlier])


def combine(lefts, pieces, masks, counts, final_shift, seqs, span, begun=None, offset=0, total=None):
    last = total is None
    pairs, depth, _ = lefts[0].shape
    rows = sum(piece.shape[0] for piece in pieces) // len(masks)
    total = total or 2 * pairs * len(lefts)
    stage = pltpu.VMEM((total // 2, 2, span, LANES), BF16)
    args = [] if begun is None else [keep(begun)]
    args += [final_shift[None], *[keep(left) for left in lefts], *pieces]
    outs = ([jax.ShapeDtypeStruct((total, span, LANES), BF16)] if last else []) + [stage]
    return pl.pallas_call(
        functools.partial(combine_kernel, seqs, rows, len(pieces), masks, counts, offset, last, 0 if begun is None else 1),
        out_shape=outs,
        in_specs=[VMEM] * len(args),
        out_specs=[HBM, VMEM] if last else [VMEM],
        input_output_aliases={} if begun is None else {0: len(outs) - 1},
        scratch_shapes=[pltpu.VMEM((rows * len(masks), depth), BF16), pltpu.SemaphoreType.DMA],
        compiler_params=params(),
        cost_estimate=pl.CostEstimate(
            flops=4 * pairs * sum(counts) * rows * LANES * depth, bytes_accessed=0, transcendentals=0
        ),
        name="combine_last" if last else "combine_some",
    )(*args)[0]


def linear(target):
    moves = []
    for r in range(16):
        for c in range(2):
            t = target(r, c, r // 8 == c)
            if t is not None:
                moves.append((r * 2 + c, t[0] * 2 + t[1]))
    return moves


def flip(value, bits):
    return lax.ppermute(value, "row", [(r, r ^ bits) for r in range(16)])


def plain(x, gain, shift, first, first_shift, second, second_shift, final, final_shift):
    seqs, here, _ = x.shape
    width = first.shape[1]
    wide = x.astype(F32)
    centered = wide - jnp.mean(wide, axis=-1, keepdims=True)
    variance = jnp.mean(centered * centered, axis=-1, keepdims=True)
    normed = (centered * lax.rsqrt(variance + 1e-05) * gain + shift).astype(BF16)
    left = (jnp.einsum("src,ck->rsk", normed, first, preferred_element_type=F32) + first_shift).astype(BF16)
    right = (jnp.einsum("src,ck->rks", normed, second, preferred_element_type=F32) + second_shift[:, None]).astype(BF16)
    right = right.reshape(here, width, seqs // RUN, RUN).transpose(0, 2, 1, 3).reshape(here, seqs * width)
    left = lax.all_gather(left.reshape(here, seqs * width), "col", axis=0, tiled=True)
    groups = LANES // width
    left = left.reshape(groups, -1, width).transpose(1, 0, 2).reshape(-1, LANES)
    every = lax.all_gather(right, ("row", "col"), axis=0, tiled=True)
    span = every.shape[0] // lax.axis_size("col")
    mine = lax.dynamic_slice_in_dim(every, lax.axis_index("col") * span, span, 0)
    spread_left, _ = spread(left, final, seqs, width)
    return combine([spread_left], [mine], (0,), (1,), final_shift, seqs, span)


def per_device(x, gain, shift, first, first_shift, second, second_shift, final, final_shift):
    seqs, here, _ = x.shape
    width = first.shape[1]
    if (lax.axis_size("row"), lax.axis_size("col"), here % 24) != (16, 2, 0):
        return plain(x, gain, shift, first, first_shift, second, second_shift, final, final_shift)
    right, left, final = project(x, gain, shift, first, first_shift, second, second_shift, final)
    both = ("row", "col")
    far = lax.ppermute(right, both, linear(lambda r, c, i: (r ^ 1, c) if i else (r ^ 8, 1 - c)))
    near = lax.ppermute(right, both, linear(lambda r, c, i: (r ^ 8, c) if i else (r, 1 - c)))
    own, pairs = spread(left, keep(final), seqs, width)
    beside = lax.ppermute(after([left], keep(pairs))[0], "col", [(0, 1), (1, 0)])
    pair = arrange(right, near, far, pairs)
    first, second, third = [flip(pair, bits) for bits in (2, 4, 6)]
    lefts = [own, spread(beside, final, seqs, width, pairs)]
    span = 16 * here
    some, masks, total = [pair, flip(pair, 1)], (0, 1), 2 * here
    begun = combine(lefts, some, masks, (2, 2), final_shift, seqs, span, None, 0, total)
    three = join([first, second, third], begun)
    begun = combine(lefts[:1], [three], (2, 4, 6), (3,), final_shift, seqs, span, begun, 0, total)
    return combine(lefts, [flip(three, 1), three], (3, 5, 7, 2, 4, 6), (3, 6), final_shift, seqs, span, begun)


def solution(mesh):
    return jax.shard_map(
        per_device,
        mesh=mesh,
        in_specs=(P("groups", ("row", "col"), None), P(), P(), P(), P(), P(), P(), P(), P()),
        out_specs=P(("groups", "row"), "col", None),
        check_vma=False,
    )
```
